256 devices in a mesh: kv: 32 (over x, z), head: 8 (over y, core).
Axes of the slice: x: 4, y: 4, z: 8, core: 2. Of those that a mesh axis runs over, the one named last changes fastest.
Arguments:
- queries: bfloat16 [256, 16384], P(None, 'head'), may hold values from -16 to 16
- cache_keys: bfloat16 [81920, 1024], P('kv', 'head'), may hold values from -5 to 5
- cache_values: bfloat16 [81920, 1024], P('kv', 'head'), may hold values from -6 to 6
- residual: bfloat16 [256, 16384], P('kv', 'head'), may hold values from -12 to 12
- norm_gain: float32 [16384], P('head'), may hold values from 0.1 to 1.9
- w_gate: bfloat16 [16384, 28672], P('head', 'kv'), may hold values from -0.046875 to 0.046875
- w_up: bfloat16 [16384, 28672], P('head', 'kv'), may hold values from -0.046875 to 0.046875
- w_down: bfloat16 [28672, 16384], P('kv', 'head'), may hold values from -0.03125 to 0.03125
Outputs:
- attended: bfloat16 [256, 16384], P('kv', 'head')
- layer_out: bfloat16 [256, 16384], P('kv', 'head')
The draws below stay inside these ranges and needn't reach their ends.
All inputs are finite; a program needn't handle non-finite values.
Results may differ from the reference program's by a relative error of at most 0.008.
Values may be sent and summed in bfloat16 or wider, within the bound.
A program may use at most 128 MiB of HBM per device.

```python
import jax
import jax.numpy as jnp
from jax import lax

HD = 128
QH = 128
KVH = 8
D = 16384
FF = 28672
ROWS = 256
CTX_DEV = 2560
CTX = 81920
N_KV = 32


def draw_queries(key, part):
    key = jax.random.fold_in(key, 11)
    return jnp.clip(jax.random.normal(key, (ROWS, QH * HD), jnp.float32) * 1.6, -6.4, 6.4).astype(jnp.bfloat16)


def draw_cache_keys(key, part):
    key = jax.random.fold_in(key, 12)
    return jnp.clip(jax.random.normal(key, (CTX, KVH * HD), jnp.float32) * 1.6, -5.0, 5.0).astype(jnp.bfloat16)


def draw_residual(key, part):
    key = jax.random.fold_in(key, 13)
    first, second, third = jax.random.split(key, 3)
    position = jnp.arange(D, dtype=jnp.float32) / D
    row_scale = jnp.exp(jax.random.uniform(second, (ROWS, 1), jnp.float32, -0.6931, 0.6931))
    col_scale = 0.03 * jnp.exp(jax.random.uniform(third, (1, D), jnp.float32, 0.0, 2.3026))
    base = jnp.clip(jax.random.normal(first, (ROWS, D), jnp.float32), -4.0, 4.0)
    trend = 3.0 ** position
    return (base * row_scale * col_scale * trend[None, :]).astype(jnp.bfloat16)


def steps_of(key, extent, pieces, low, top_value):
    loudness, own = 1.0, jax.random.fold_in(key, 6)
    for axis_at, parts in pieces:
        draws = jnp.exp(jax.random.uniform(jax.random.fold_in(own, axis_at), (parts,), jnp.float32, low / len(pieces), top_value / len(pieces)))
        loudness = loudness * jnp.repeat(draws, extent[axis_at] // parts).reshape([-1 if axis == axis_at else 1 for axis in range(len(extent))])
    return loudness


def noise(key, extent, spread, reach, cuts=(), kind=jnp.bfloat16):
    result = spread * jax.random.normal(key, extent, jnp.float32)
    if cuts:
        result = result * steps_of(key, extent, cuts, -0.22, 0.18)
    return jnp.clip(result, -reach, reach).astype(kind)


def setup_inputs(seed: int = 0) -> dict:
    keys = jax.random.split(jax.random.key(seed), 9)
    return {
        "queries": draw_queries(jax.random.fold_in(keys[8], 71), 0),
        "cache_keys": draw_cache_keys(jax.random.fold_in(keys[8], 71), 0),
        "cache_values": noise(keys[2], (CTX, KVH * HD), 1.0, 6.0, ((0, 32), (1, 8))),
        "residual": draw_residual(jax.random.fold_in(keys[8], 71), 0),
        "norm_gain": jnp.clip(1.0 + 0.18 * jax.random.normal(keys[4], (D,), jnp.float32), 0.1, 1.9),
        "w_gate": noise(keys[5], (D, FF), D ** -0.5, 0.046875, ((0, 8), (1, 32))),
        "w_up": noise(keys[6], (D, FF), D ** -0.5, 0.046875, ((0, 8), (1, 32))),
        "w_down": noise(keys[7], (FF, D), FF ** -0.5, 0.03125, ((0, 32), (1, 8))),
    }


def reference(queries, cache_keys, cache_values, residual, norm_gain, w_gate, w_up, w_down):
    group_size = QH // KVH
    score_scale = HD ** (-0.5)
    key_blocks = cache_keys.reshape(N_KV, CTX_DEV, KVH, HD)
    value_blocks = cache_values.reshape(N_KV, CTX_DEV, KVH, HD)

    def one_group(group_idx):
        query_block = lax.dynamic_slice_in_dim(queries, group_idx * group_size * HD, group_size * HD, 1)
        query_block = query_block.reshape(ROWS * group_size, HD)

        def one_block(block_idx):
            key_part = key_blocks[block_idx, :, group_idx, :]
            value_part = value_blocks[block_idx, :, group_idx, :]
            scores = jnp.dot(query_block, key_part.T, preferred_element_type=jnp.float32) * score_scale
            peak = lax.optimization_barrier(jnp.max(scores, axis=1))
            expd = jnp.exp(scores - peak[:, None])
            total = lax.optimization_barrier(jnp.sum(expd, axis=1))
            partial_out = jnp.dot(expd.astype(jnp.bfloat16), value_part, preferred_element_type=jnp.float32)
            return (peak, total, partial_out)
        peaks, totals, outs = lax.map(one_block, jnp.arange(N_KV, dtype=jnp.int32))
        row_top = lax.optimization_barrier(jnp.max(peaks, axis=0))
        factor = jnp.exp(peaks - row_top[None])
        numer = lax.optimization_barrier(jnp.sum(outs * factor[:, :, None], axis=0))
        denom = lax.optimization_barrier(jnp.sum(totals * factor, axis=0))
        return (numer / denom[:, None]).reshape(ROWS, group_size * HD)
    per_group = lax.map(one_group, jnp.arange(KVH, dtype=jnp.int32))
    attended = jnp.transpose(per_group, (1, 0, 2)).reshape(ROWS, QH * HD).astype(jnp.bfloat16)
    stream = residual.astype(jnp.float32) + attended.astype(jnp.float32)
    squares = lax.optimization_barrier(jnp.sum(stream * stream, axis=1))
    normed = (stream * lax.rsqrt(squares / D + 1e-05)[:, None] * norm_gain[None, :]).astype(jnp.bfloat16)
    gate = jnp.dot(normed, w_gate, preferred_element_type=jnp.float32)
    upward = jnp.dot(normed, w_up, preferred_element_type=jnp.float32)
    hidden = (jax.nn.silu(gate) * upward).astype(jnp.bfloat16)
    layer_out = (stream + jnp.dot(hidden, w_down, preferred_element_type=jnp.float32)).astype(jnp.bfloat16)
    return (attended, layer_out)
```

```python
import jax
import jax.numpy as jnp
from jax import lax
from jax.experimental import pallas as pl
from jax.experimental.pallas import tpu as pltpu
from jax.sharding import PartitionSpec as P

MESH = pl.DeviceIdType.MESH
f32, bf16 = jnp.float32, jnp.bfloat16
HD = 128
D = 16384
EPSILON = 1e-05
NX, NZ, NY = 4, 8, 4
NKV = NX * NZ
OWN = 8
CTX = 2560
LOCAL = 2048
UNITS = 896
KC = 512
SCALE = float(HD**-0.5 * 1.4426950408889634)
PIECE = 144
FCH = UNITS // 128
DCH = 4
DCW = LOCAL // DCH
Z_ORDER = (1, 7, 2, 6, 3, 5, 4)


def split2(v):
    hi = v.astype(bf16).astype(f32)
    return hi, v - hi


def split3(v):
    hi, rest = split2(v)
    mid, low = split2(rest)
    return hi, mid, low


def stats_rows(peak, total):
    width = peak.shape[1]
    rows = [*split3(peak), *split2(total), jnp.zeros((11, width), f32)]
    return jnp.concatenate(rows, axis=0).astype(bf16)


def read_stats(ref):
    s = ref[128:PIECE, :].astype(f32)
    return s[0:1] + s[1:2] + s[2:3], s[3:4] + s[4:5]


def wait_bytes(ref, sem):
    pltpu.make_async_copy(ref, ref, sem).wait()


def kernel(
    q, k, v, res, gain, wg, wu, wd, att_out, out,
    vt, qs, sc, sbuf, xbuf, zs, zbuf, stream, ag, xn, ssb, ssr, wgu, wdv,
    gacc, gs, cbuf, ys, yb, hid, dsf, ds, dxb, zs2, dzb,
    w_sem, d_sem, ax_s, ax_r, az_s, az_r, gz_s, gz_r, gx_s, gx_r,
    ss_s, ss_r, c_s, c_r, y_s, y_r, hy_s, hy_r, hc_s, hc_r, dx_s, dx_r, dz_s, dz_r,
):
    kv, hd = lax.axis_index("kv"), lax.axis_index("head")
    x, z = kv // NZ, kv % NZ
    y, c = hd // 2, hd % 2

    def at_x(dx):
        return (((x + dx) % NX) * NZ + z, hd)

    def at_z(o):
        return (x * NZ + (z + o) % NZ, hd)

    def at_y(dy):
        return (kv, ((y + dy) % NY) * 2 + c)

    def at_head(o):
        return (kv, (hd + o) % 8)

    other = (kv, y * 2 + 1 - c)

    def remote(src, dst, send, recv, dev):
        return pltpu.make_async_remote_copy(
            src_ref=src, dst_ref=dst, send_sem=send, recv_sem=recv, device_id=dev, device_id_type=MESH
        )

    for j in range(FCH):
        cols = pl.ds(j * 128, 128)
        pltpu.make_async_copy(wg.at[:, cols], wgu.at[j, :, pl.ds(0, 128)], w_sem).start()
        pltpu.make_async_copy(wu.at[:, cols], wgu.at[j, :, pl.ds(128, 128)], w_sem).start()
    for j in range(DCH):
        pltpu.make_async_copy(wd.at[:, pl.ds(j * DCW, DCW)], wdv.at[j], d_sem).start()

    barrier = pltpu.get_barrier_semaphore()
    peers = [at_x(o) for o in range(1, NX)] + [at_z(o) for o in range(1, NZ)] + [at_head(o) for o in range(1, 8)]
    for dev in peers:
        pl.semaphore_signal(barrier, inc=1, device_id=dev, device_id_type=MESH)

    vt[...] = v[...].astype(f32).T.astype(bf16)

    def arrange(i, _):
        rows = q[pl.ds(pl.multiple_of(i * 16, 16), 16), :].astype(f32)
        for d in range(2):
            tiles = [rows[8 * d : 8 * d + 8, 128 * h : 128 * h + 128] for h in range(16)]
            qs[2 * i + d] = jnp.concatenate(tiles, axis=0).astype(bf16)
        return 0

    lax.fori_loop(0, NKV // 2, arrange, 0)

    def z_to(j):
        d = (j + 1) // 2
        return (z + 4 + d * (1 - 2 * (j % 2))) % NZ

    def pair_of(half):
        return (2, 1) if half == 0 else (3, 0)

    def queries_of(j, half):
        a, b = pair_of(half)
        zt = z_to(j)
        return jnp.concatenate([qs[((x + a) % NX) * NZ + zt], qs[((x + b) % NX) * NZ + zt]], axis=0)

    def scores(i, qb, slot):
        rows = pl.ds(i * KC, KC)
        s = lax.dot_general(k[rows, :], qb, (((1,), (1,)), ((), ())), preferred_element_type=f32)
        sc[slot, rows, :] = s
        return jnp.max(s.reshape(KC // 8, 8, 256), axis=0)

    def add(a, b):
        return b if a is None else a + b

    def both(j, half, top, qb):
        peak = jnp.max(top, axis=0, keepdims=True) * SCALE
        acc = total = following = None
        for i in range(CTX // KC):
            rows = pl.ds(i * KC, KC)
            p = jnp.exp2(sc[half, rows, :] * SCALE - peak)
            total = add(total, jnp.sum(p.reshape(KC // 8, 8, 256), axis=0))
            acc = add(acc, jnp.dot(vt[:, rows], p.astype(bf16), preferred_element_type=f32))
            m = scores(i, qb, 1 - half)
            following = m if following is None else jnp.maximum(following, m)
        total = jnp.sum(total, axis=0, keepdims=True)
        acc = acc.astype(bf16)
        stats = stats_rows(peak, total)
        for n, dx in enumerate(pair_of(half)):
            sbuf[dx, j, :128, :] = acc[:, n * 128 : n * 128 + 128]
            sbuf[dx, j, 128:PIECE, :] = stats[:, n * 128 : n * 128 + 128]
        for dx in pair_of(half):
            if dx:
                remote(sbuf.at[dx, j], xbuf.at[dx - 1, j], ax_s, ax_r.at[dx - 1, j], at_x(dx)).start()
        return following

    def merge(refs):
        stats = [read_stats(r) for r in refs]
        peak = stats[0][0]
        for m, _ in stats[1:]:
            peak = jnp.maximum(peak, m)
        factors = [jnp.exp2(m - peak) for m, _ in stats]
        total = None
        for f, (_, t) in zip(factors, stats):
            total = add(total, f * t)
        return peak, total, factors

    def weighted(refs, weights):
        acc = None
        for r, w in zip(refs, weights):
            acc = add(acc, r[:128, :].astype(f32) * w)
        return acc

    def send_z(g):
        return remote(zs.at[g], zbuf.at[g], az_s, az_r.at[g], (x * NZ + z_to(g), hd))

    def combine(g):
        for dx in range(1, NX):
            remote(sbuf.at[dx, g], xbuf.at[dx - 1, g], ax_s, ax_r.at[dx - 1, g], at_x(dx)).wait_recv()
        refs = [sbuf.at[0, g]] + [xbuf.at[n, g] for n in range(NX - 1)]
        peak, total, factors = merge(refs)
        zs[g, :128, :] = weighted(refs, factors).astype(bf16)
        zs[g, 128:PIECE, :] = stats_rows(peak, total)

    first = queries_of(0, 0)
    top = None
    for i in range(CTX // KC):
        m = scores(i, first, 0)
        top = m if top is None else jnp.maximum(top, m)

    pl.semaphore_wait(barrier, len(peers))

    def attend(j, top):
        top = both(j, 0, top, queries_of(j, 1))
        top = both(j, 1, top, queries_of((j + 1) % NZ, 0))

        @pl.when(j >= 2)
        def _():
            combine(j - 2)
            send_z(j - 2).start()

        return top

    lax.fori_loop(0, NZ, attend, top)
    combine(6)
    send_z(6).start()
    combine(7)
    for g in range(NZ - 1):
        send_z(g).wait_recv()
    refs = [zs.at[NZ - 1]] + [zbuf.at[g] for g in range(NZ - 1)]
    peak, total, factors = merge(refs)
    inv = 1.0 / total
    att = weighted(refs, [f * inv for f in factors]).T
    att = jnp.concatenate([att[8 * h : 8 * h + 8, :] for h in range(16)], axis=1).astype(bf16)
    att_out[...] = att

    st = res[...].astype(f32) + att.astype(f32)
    stream[...] = st
    squares = jnp.broadcast_to(jnp.sum(st * st, axis=1, keepdims=True), (OWN, 128))
    t = st * gain[...]
    ag[kv, :128, :] = jnp.concatenate([t[:, 128 * h : 128 * h + 128] for h in range(16)], axis=0).astype(bf16)
    ag[kv, 128:PIECE, :] = jnp.concatenate(split2(squares), axis=0).astype(bf16)

    def gather_z(o):
        return remote(ag.at[kv], ag.at[kv], gz_s, gz_r.at[o - 1], at_z(o))

    def gather_x(src, dx):
        return remote(ag.at[src], ag.at[src], gx_s, gx_r.at[dx - 1], at_x(dx))

    for o in reversed(Z_ORDER):
        gather_z(o).start()
    for dx in (2, 1, 3):
        gather_x(kv, dx).start()
    for o in Z_ORDER:
        src = x * NZ + (z + NZ - o) % NZ
        remote(ag.at[src], ag.at[src], gz_s, gz_r.at[o - 1], at_z(o)).wait_recv()
        for dx in (2, 1, 3):
            gather_x(src, dx).start()
    for dx in range(1, NX):
        wait_bytes(ag.at[pl.ds(((x + NX - dx) % NX) * NZ, NZ)], gx_r.at[dx - 1])

    def rebuild(i, _):
        a = ag[2 * i].astype(f32)
        b = ag[2 * i + 1].astype(f32)
        rows = pl.ds(pl.multiple_of(i * 16, 16), 16)
        for h in range(16):
            tile = jnp.concatenate([a[8 * h : 8 * h + 8], b[8 * h : 8 * h + 8]], axis=0)
            xn[rows, 128 * h : 128 * h + 128] = tile.astype(bf16)
        ssb[rows, :] = jnp.concatenate([a[128:136] + a[136:144], b[128:136] + b[136:144]], axis=0)
        return 0

    lax.fori_loop(0, NKV // 2, rebuild, 0)

    def square_copy(o):
        to = (hd + o) % 8
        block = (to % 2) * NY + to // 2
        return remote(
            ssb.at[pl.ds(pl.multiple_of(block * 32, 32), 32)], ssr.at[o - 1], ss_s, ss_r.at[o - 1], at_head(o)
        )

    for o in range(1, 8):
        square_copy(o).start()

    wait_bytes(wgu, w_sem)
    mine = pl.ds(pl.multiple_of(c * 128, 128), 128)
    theirs = pl.ds(pl.multiple_of((1 - c) * 128, 128), 128)
    block = c * NY + y
    own32 = pl.ds(pl.multiple_of(block * 32, 32), 32)

    def core_copy(j):
        return remote(gs.at[j], cbuf.at[j], c_s, c_r.at[j], other)

    def sum_cores(j):
        core_copy(j).wait_recv()
        s = gacc[j, mine, :] + cbuf[j].astype(f32)
        gacc[j, mine, :] = s
        ys[j] = s.astype(bf16).reshape(NY, 32, 256)
        for dy in (2, 1, 3):
            remote(ys.at[j, (y + dy) % NY], yb.at[dy - 1, j], y_s, y_r.at[dy - 1], at_y(dy)).start()

    def project(j, _):
        gacc[j] = jnp.dot(xn[...], wgu[j], preferred_element_type=f32)
        gs[j] = gacc[j, theirs, :].astype(bf16)
        core_copy(j).start()

        @pl.when(j >= 3)
        def _():
            sum_cores(j - 3)

        return 0

    lax.fori_loop(0, FCH, project, 0)
    for j in range(FCH - 3, FCH):
        sum_cores(j)
    for o in range(1, 8):
        square_copy(o).wait_recv()
    squares = ssb[own32, :]
    for o in range(7):
        squares = squares + ssr[o]
    scale = lax.rsqrt(squares / D + EPSILON)
    for dy in range(1, NY):
        wait_bytes(yb.at[dy - 1], y_r.at[dy - 1])
    for j in range(FCH):
        s = gacc[j, own32, :]
        for n in range(NY - 1):
            s = s + yb[n, j].astype(f32)
        gate = s[:, :128] * scale
        up = s[:, 128:] * scale
        hid[own32, 128 * j : 128 * j + 128] = (gate / (1.0 + jnp.exp(-gate)) * up).astype(bf16)

    def rows_of(yy, cc):
        return hid.at[pl.ds(pl.multiple_of((cc * NY + yy) * 32, 32), 32)]

    for dy in (2, 1, 3):
        remote(rows_of(y, c), rows_of(y, c), hy_s, hy_r.at[dy - 1], at_y(dy)).start()
    remote(rows_of(y, c), rows_of(y, c), hc_s, hc_r, other).start()
    for dy in (1, 3, 2):
        piece = rows_of((y + NY - dy) % NY, c)
        remote(piece, piece, hy_s, hy_r.at[dy - 1], at_y(dy)).wait_recv()
        remote(piece, piece, hc_s, hc_r, other).start()
    wait_bytes(hid.at[theirs], hc_r)

    wait_bytes(wdv, d_sem)

    def down_x(j, dx):
        return remote(ds.at[j, (x + dx) % NX], dxb.at[dx - 1, j], dx_s, dx_r.at[dx - 1, j], at_x(dx))

    def down(j, _):
        acc = jnp.dot(hid[...], wdv[j], preferred_element_type=f32)
        for h in range(DCW // 128):
            dsf[:, h] = acc[:, 128 * h : 128 * h + 128].reshape(NKV, OWN, 128)
        ds[j] = dsf[...].reshape(NX, NZ * 32, 128).astype(bf16)
        for dx in (2, 1, 3):
            down_x(j, dx).start()
        return 0

    lax.fori_loop(0, DCH, down, 0)

    def sum_x(j, _):
        for dx in range(1, NX):
            down_x(j, dx).wait_recv()
        s = ds[j, x].astype(f32)
        for n in range(NX - 1):
            s = s + dxb[n, j].astype(f32)
        zs2[j] = s.astype(bf16).reshape(NZ, 32, 128)
        for o in reversed(Z_ORDER):
            remote(zs2.at[j, (z + o) % NZ], dzb.at[o - 1, j], dz_s, dz_r.at[o - 1], at_z(o)).start()
        return 0

    lax.fori_loop(0, DCH, sum_x, 0)
    for o in range(1, NZ):
        wait_bytes(dzb.at[o - 1], dz_r.at[o - 1])
    for j in range(DCH):
        s = zs2[j, z].astype(f32)
        for n in range(NZ - 1):
            s = s + dzb[n, j].astype(f32)
        s = jnp.concatenate([s[8 * h : 8 * h + 8] for h in range(DCW // 128)], axis=1)
        cols = slice(j * DCW, j * DCW + DCW)
        out[:, cols] = (stream[:, cols] + s).astype(bf16)

    wait_bytes(sbuf.at[pl.ds(1, 3)], ax_s)
    wait_bytes(zs.at[pl.ds(0, 7)], az_s)
    wait_bytes(ag.at[pl.ds(0, 7)], gz_s)
    wait_bytes(ag.at[pl.ds(0, 24)], gx_s)
    wait_bytes(ssr, ss_s)
    wait_bytes(gs, c_s)
    wait_bytes(yb, y_s)
    wait_bytes(hid.at[pl.ds(0, 96)], hy_s)
    wait_bytes(hid.at[pl.ds(0, 128)], hc_s)
    wait_bytes(dxb, dx_s)
    wait_bytes(dzb, dz_s)


def body(queries, cache_keys, cache_values, residual, norm_gain, w_gate, w_up, w_down):
    vmem = pl.BlockSpec(memory_space=pltpu.VMEM)
    hbm = pl.BlockSpec(memory_space=pl.ANY)
    dma = pltpu.SemaphoreType.DMA
    shape = jax.ShapeDtypeStruct((OWN, LOCAL), bf16)
    scratch = [
        pltpu.VMEM((HD, CTX), bf16),
        pltpu.VMEM((NKV, 128, HD), bf16),
        pltpu.VMEM((2, CTX, 256), f32),
        pltpu.VMEM((NX, NZ, PIECE, 128), bf16),
        pltpu.VMEM((NX - 1, NZ, PIECE, 128), bf16),
        pltpu.VMEM((NZ, PIECE, 128), bf16),
        pltpu.VMEM((NZ - 1, PIECE, 128), bf16),
        pltpu.VMEM((OWN, LOCAL), f32),
        pltpu.VMEM((NKV, PIECE, 128), bf16),
        pltpu.VMEM((256, LOCAL), bf16),
        pltpu.VMEM((256, 128), f32),
        pltpu.VMEM((7, 32, 128), f32),
        pltpu.VMEM((FCH, LOCAL, 256), bf16),
        pltpu.VMEM((DCH, UNITS, DCW), bf16),
        pltpu.VMEM((FCH, 256, 256), f32),
        pltpu.VMEM((FCH, 128, 256), bf16),
        pltpu.VMEM((FCH, 128, 256), bf16),
        pltpu.VMEM((FCH, NY, 32, 256), bf16),
        pltpu.VMEM((NY - 1, FCH, 32, 256), bf16),
        pltpu.VMEM((256, UNITS), bf16),
        pltpu.VMEM((NKV, DCW // 128, OWN, 128), f32),
        pltpu.VMEM((DCH, NX, NZ * 32, 128), bf16),
        pltpu.VMEM((NX - 1, DCH, NZ * 32, 128), bf16),
        pltpu.VMEM((DCH, NZ, 32, 128), bf16),
        pltpu.VMEM((NZ - 1, DCH, 32, 128), bf16),
        dma, dma,
        dma, dma((NX - 1, NZ)),
        dma, dma((NZ - 1,)),
        dma, dma((NZ - 1,)),
        dma, dma((NX - 1,)),
        dma, dma((7,)),
        dma, dma((FCH,)),
        dma, dma((NY - 1,)),
        dma, dma((NY - 1,)),
        dma, dma,
        dma, dma((NX - 1, DCH)),
        dma, dma((NZ - 1,)),
    ]
    return pl.pallas_call(
        kernel,
        out_shape=(shape, shape),
        in_specs=[vmem] * 5 + [hbm] * 3,
        out_specs=(vmem, vmem),
        scratch_shapes=scratch,
        name="layer",
        compiler_params=pltpu.CompilerParams(
            collective_id=0, has_side_effects=True, vmem_limit_bytes=56 * 2**20
        ),
    )(
        queries, cache_keys, cache_values, residual, norm_gain.reshape(1, LOCAL), w_gate, w_up, w_down
    )


def solution(mesh):
    in_specs = (
        P(None, "head"),
        P("kv", "head"),
        P("kv", "head"),
        P("kv", "head"),
        P("head"),
        P("head", "kv"),
        P("head", "kv"),
        P("kv", "head"),
    )
    out_specs = (P("kv", "head"), P("kv", "head"))
    return jax.shard_map(body, mesh=mesh, in_specs=in_specs, out_specs=out_specs, check_vma=False)
```

```python
import jax
import jax.numpy as jnp
from jax import lax
from jax.experimental import pallas as pl
from jax.experimental.pallas import tpu as pltpu
from jax.sharding import PartitionSpec as P

MESH = pl.DeviceIdType.MESH
f32, bf16 = jnp.float32, jnp.bfloat16
HD = 128
D = 16384
EPSILON = 1e-05
NX, NZ, NY = 4, 8, 4
NKV = NX * NZ
OWN = 8
CTX = 2560
LOCAL = 2048
UNITS = 896
KC = 256
X_ORDER = (2, 1, 3, 0)
COLS = NX * 128
SCALE = float(HD**-0.5 * 1.4426950408889634)
PIECE = 144
FCH = UNITS // 128
DCH = 4
DCW = LOCAL // DCH
I_ORDER = (0, 3, 1, 2)


def split2(v):
    hi = v.astype(bf16).astype(f32)
    return hi, v - hi


def split3(v):
    hi, rest = split2(v)
    mid, low = split2(rest)
    return hi, mid, low


def stats_rows(peak, total):
    width = peak.shape[1]
    rows = [*split3(peak), *split2(total), jnp.zeros((11, width), f32)]
    return jnp.concatenate(rows, axis=0).astype(bf16)


def read_stats(ref):
    s = ref[128:PIECE, :].astype(f32)
    return s[0:1] + s[1:2] + s[2:3], s[3:4] + s[4:5]


def wait_bytes(ref, sem):
    pltpu.make_async_copy(ref, ref, sem).wait()


def kernel(
    q, k, v, res, gain, wg, wu, wd, att_out, out,
    vt, sc, sbuf, xbuf, zs, zbuf, stream, ag, xn, ssb, ssc, ssr, wgu, wdv,
    gacc, gs, cbuf, ys, yb, hid, dsf, ds, dxb, zs2, dzb,
    w_sem, d_sem, ax_s, ax_r, az_s, az_r, gz_s, gz_r, gx_s, gx_r, gf_r,
    sc_s, sc_r, ss_s, ss_r, c_s, c_r, y_s, y_r, hy_s, hy_r, hc_s, hc_r, dx_s, dx_r, dz_s, dz_r,
):
    kv, hd = lax.axis_index("kv"), lax.axis_index("head")
    x, z = kv // NZ, kv % NZ
    y, c = hd // 2, hd % 2

    def at_x(dx):
        return (((x + dx) % NX) * NZ + z, hd)

    def at_z(o):
        return (x * NZ + (z + o) % NZ, hd)

    def at_y(dy):
        return (kv, ((y + dy) % NY) * 2 + c)

    other = (kv, y * 2 + 1 - c)

    def remote(src, dst, send, recv, dev):
        return pltpu.make_async_remote_copy(
            src_ref=src, dst_ref=dst, send_sem=send, recv_sem=recv, device_id=dev, device_id_type=MESH
        )

    for j in range(FCH):
        cols = pl.ds(j * 128, 128)
        pltpu.make_async_copy(wg.at[:, cols], wgu.at[j, :, pl.ds(0, 128)], w_sem).start()
        pltpu.make_async_copy(wu.at[:, cols], wgu.at[j, :, pl.ds(128, 128)], w_sem).start()
    for j in range(DCH):
        pltpu.make_async_copy(wd.at[:, pl.ds(j * DCW, DCW)], wdv.at[j], d_sem).start()

    barrier = pltpu.get_barrier_semaphore()
    peers = [at_x(o) for o in range(1, NX)] + [at_z(o) for o in range(1, NZ)] + [at_y(o) for o in range(1, NY)] + [other]
    for dev in peers:
        pl.semaphore_signal(barrier, inc=1, device_id=dev, device_id_type=MESH)

    vt[:HD] = v[...].astype(f32).T.astype(bf16)
    vt[HD:] = jnp.ones((16, CTX), bf16)

    def z_off(j):
        i = j % 4
        same = jnp.where(i == 0, 4, jnp.where(i == 1, 2, jnp.where(i == 2, 6, 0)))
        cross = jnp.where(i == 0, 3, jnp.where(i == 1, 5, jnp.where(i == 2, 1, 7)))
        return jnp.where((z + j // 4) % 2 == 0, same, cross)

    def z_to(j):
        return (z + z_off(j)) % NZ

    def queries_of(j):
        zt = z_to(j)
        tiles = []
        for dx in X_ORDER:
            owner = ((x + dx) % NX) * NZ + zt
            rows = q[pl.ds(pl.multiple_of(owner // 2 * 16, 16), 16), :].astype(f32)
            rows = jnp.where(zt % 2 == 0, rows[:8], rows[8:])
            tiles += [rows[:, 128 * h : 128 * h + 128] for h in range(16)]
        return jnp.concatenate(tiles, axis=0).astype(bf16)

    def scores(i, qb, top):
        rows = pl.ds(i * KC, KC)
        s = lax.dot_general(k[rows, :], qb, (((1,), (1,)), ((), ())), preferred_element_type=f32)
        sc[rows, :] = s
        m = jnp.max(s.reshape(KC // 8, 8, COLS), axis=0)
        return m if top is None else jnp.maximum(top, m)

    def add(a, b):
        return b if a is None else a + b

    def step(j, top):
        qb = queries_of((j + 1) % NZ)
        peak = jnp.max(top, axis=0, keepdims=True) * SCALE
        acc = following = None
        for i in range(CTX // KC):
            rows = pl.ds(i * KC, KC)
            p = jnp.exp2(sc[rows, :] * SCALE - peak)
            acc = add(acc, jnp.dot(vt[:, rows], p.astype(bf16), preferred_element_type=f32))
            following = scores(i, qb, following)
        stats = stats_rows(peak, acc[HD : HD + 1])
        acc = acc[:HD].astype(bf16)
        for n, dx in enumerate(X_ORDER):
            cols = slice(n * 128, n * 128 + 128)
            sbuf[dx, j, :HD, :] = acc[:, cols]
            sbuf[dx, j, HD:PIECE, :] = stats[:, cols]
        for dx in X_ORDER[:3]:
            remote(sbuf.at[dx, j], xbuf.at[dx - 1, j], ax_s, ax_r.at[dx - 1, j], at_x(dx)).start()
        return following

    def merge(refs):
        stats = [read_stats(r) for r in refs]
        peak = stats[0][0]
        for m, _ in stats[1:]:
            peak = jnp.maximum(peak, m)
        factors = [jnp.exp2(m - peak) for m, _ in stats]
        total = None
        for f, (_, t) in zip(factors, stats):
            total = add(total, f * t)
        return peak, total, factors

    def weighted(refs, weights):
        acc = None
        for r, w in zip(refs, weights):
            acc = add(acc, r[:128, :].astype(f32) * w)
        return acc

    def combine(g):
        for dx in range(1, NX):
            remote(sbuf.at[dx, g], xbuf.at[dx - 1, g], ax_s, ax_r.at[dx - 1, g], at_x(dx)).wait_recv()
        refs = [sbuf.at[0, g]] + [xbuf.at[n, g] for n in range(NX - 1)]
        peak, total, factors = merge(refs)
        zs[g, :128, :] = weighted(refs, factors).astype(bf16)
        zs[g, 128:PIECE, :] = stats_rows(peak, total)
        off = z_off(g)

        @pl.when(off != 0)
        def _():
            remote(zs.at[g], zbuf.at[off - 1], az_s, az_r.at[off - 1], at_z(off)).start()

    first = queries_of(0)
    top = None
    for i in range(CTX // KC):
        top = scores(i, first, top)

    pl.semaphore_wait(barrier, len(peers))

    def attend(j, top):
        top = step(j, top)

        @pl.when(j >= 2)
        def _():
            combine(j - 2)

        return top

    lax.fori_loop(0, NZ, attend, top)

    def gather_z(o):
        return remote(ag.at[kv], ag.at[kv], gz_s, gz_r.at[o - 1], at_z(o))

    def finish_merge(p):
        @pl.when(z % 2 == p)
        def _():
            for o in range(1, NZ):
                remote(zs.at[0], zbuf.at[o - 1], az_s, az_r.at[o - 1], at_z(o)).wait_recv()
            refs = [zs.at[4 * p + 3]] + [zbuf.at[n] for n in range(NZ - 1)]
            _, total, factors = merge(refs)
            inv = 1.0 / total
            att = weighted(refs, [f * inv for f in factors]).T
            att = jnp.concatenate([att[8 * h : 8 * h + 8, :] for h in range(16)], axis=1).astype(bf16)
            att_out[...] = att
            st = res[...].astype(f32) + att.astype(f32)
            stream[...] = st
            squares = jnp.broadcast_to(jnp.sum(st * st, axis=1, keepdims=True), (OWN, 128))
            t = st * gain[...]
            rows = jnp.concatenate([t[:, 128 * h : 128 * h + 128] for h in range(16)], axis=0)
            ag[kv, :128, :] = rows.astype(bf16)
            ag[kv, 128:PIECE, :] = jnp.concatenate(split2(squares), axis=0).astype(bf16)
            for o in (4, 5, 3, 6, 2, 7, 1):
                gather_z(o).start()

    def gather_x(src, dx, recv):
        return remote(ag.at[src], ag.at[src], gx_s, recv, at_x(dx))

    def source(p, i):
        o = 2 * i + (z + p) % 2
        return o, (z + NZ - o) % NZ

    def spread(p, i):
        o, zo = source(p, i)
        src = x * NZ + zo

        @pl.when(o != 0)
        def _():
            remote(ag.at[src], ag.at[src], gz_s, gz_r.at[o - 1], at_z(o)).wait_recv()

        for n, dx in enumerate((1, 3)):
            gather_x(src, dx, gx_r.at[n, o]).start()

    def forward(p, i):
        n, dx = ((0, 1), (1, 3))[i % 2]
        o, zo = source(p, i)
        src = ((x + NX - dx) % NX) * NZ + zo
        gather_x(src, dx, gx_r.at[n, o]).wait_recv()
        gather_x(src, dx, gf_r.at[p, n]).start()

    def gathered(p):
        for i in I_ORDER:
            n, dx = ((1, 3), (0, 1))[i % 2]
            o, zo = source(p, i)
            gather_x(((x + NX - dx) % NX) * NZ + zo, dx, gx_r.at[n, o]).wait_recv()
        for n in range(2):
            wait_bytes(ag.at[pl.ds(0, 2)], gf_r.at[p, n])

    def rebuild(p):
        def pair(i, _):
            first = (i // 2) * NZ + 4 * (i % 2) + p
            a = ag[first].astype(f32)
            b = ag[first + 2].astype(f32)
            rows = pl.ds(pl.multiple_of(i * 16, 16), 16)
            for h in range(16):
                tile = jnp.concatenate([a[8 * h : 8 * h + 8], b[8 * h : 8 * h + 8]], axis=0)
                xn[p, rows, 128 * h : 128 * h + 128] = tile.astype(bf16)
            ssb[p, rows, :] = jnp.concatenate([a[128:136] + a[136:144], b[128:136] + b[136:144]], axis=0)
            return 0

        lax.fori_loop(0, 8, pair, 0)

    mine = pl.ds(pl.multiple_of(c * 64, 64), 64)
    theirs = pl.ds(pl.multiple_of((1 - c) * 64, 64), 64)

    def rows_at(yy, cc):
        return pl.ds(pl.multiple_of((cc * NY + yy) * 16, 16), 16)

    own16 = rows_at(y, c)

    def square_core(p):
        return remote(ssb.at[p, theirs], ssc.at[p], sc_s, sc_r.at[p], other)

    def square_y(p, dy):
        src = ssb.at[p, rows_at((y + dy) % NY, c)]
        return remote(src, ssr.at[p, dy - 1], ss_s, ss_r.at[p, dy - 1], at_y(dy))

    def core_copy(p, j):
        return remote(gs.at[p, j], cbuf.at[p, j], c_s, c_r.at[p, j], other)

    def project(p):
        square_core(p).start()

        def chunk(j, _):
            gacc[p, j] = jnp.dot(xn[p], wgu[j], preferred_element_type=f32)
            gs[p, j] = gacc[p, j, theirs, :].astype(bf16)
            core_copy(p, j).start()
            return 0

        lax.fori_loop(0, FCH, chunk, 0)

    def sum_cores(p):
        square_core(p).wait_recv()
        ssb[p, mine, :] = ssb[p, mine, :] + ssc[p]
        for dy in (2, 1, 3):
            square_y(p, dy).start()

        def chunk(j, _):
            core_copy(p, j).wait_recv()
            s = gacc[p, j, mine, :] + cbuf[p, j].astype(f32)
            gacc[p, j, mine, :] = s
            ys[p, j] = s.astype(bf16).reshape(NY, 16, 256)
            for dy in (2, 1, 3):
                to = (y + dy) % NY
                remote(ys.at[p, j, to], yb.at[p, dy - 1, j], y_s, y_r.at[p, dy - 1], at_y(dy)).start()
            return 0

        lax.fori_loop(0, FCH, chunk, 0)

    def hid_rows(p, yy):
        return hid.at[p, rows_at(yy, c)]

    def hid_y(p, yy, dy):
        return remote(hid_rows(p, yy), hid_rows(p, yy), hy_s, hy_r.at[p, dy - 1], at_y(dy))

    def hid_core(p, yy):
        return remote(hid_rows(p, yy), hid_rows(p, yy), hc_s, hc_r.at[p], other)

    def activate(p):
        for dy in range(1, NY):
            square_y(p, dy).wait_recv()
        squares = ssb[p, own16, :]
        for n in range(NY - 1):
            squares = squares + ssr[p, n]
        scale = lax.rsqrt(squares / D + EPSILON)
        for dy in range(1, NY):
            wait_bytes(yb.at[p, dy - 1], y_r.at[p, dy - 1])
        for j in range(FCH):
            s = gacc[p, j, own16, :]
            for n in range(NY - 1):
                s = s + yb[p, n, j].astype(f32)
            gate = s[:, :128] * scale
            up = s[:, 128:] * scale
            hid[p, own16, 128 * j : 128 * j + 128] = (gate / (1.0 + jnp.exp(-gate)) * up).astype(bf16)
        for dy in (2, 1, 3):
            hid_y(p, y, dy).start()
        hid_core(p, y).start()

    def hid_forward(p):
        for dy in (1, 3, 2):
            yy = (y + NY - dy) % NY
            hid_y(p, yy, dy).wait_recv()
            hid_core(p, yy).start()

    def down_x(p, j, dx):
        src = ds.at[p, j, (x + dx) % NX]
        return remote(src, dxb.at[p, dx - 1, j], dx_s, dx_r.at[p, dx - 1, j], at_x(dx))

    def down(p):
        wait_bytes(hid.at[p, theirs], hc_r.at[p])

        def chunk(j, _):
            acc = jnp.dot(hid[p], wdv[j], preferred_element_type=f32)
            for h in range(DCW // 128):
                dsf[:, h] = acc[:, 128 * h : 128 * h + 128].reshape(NKV // 2, OWN, 128)
            ds[p, j] = dsf[...].reshape(NX, 128, 128).astype(bf16)
            for dx in (2, 1, 3):
                down_x(p, j, dx).start()
            return 0

        lax.fori_loop(0, DCH, chunk, 0)

    def sum_x(p):
        def chunk(j, _):
            for dx in range(1, NX):
                down_x(p, j, dx).wait_recv()
            s = ds[p, j, x].astype(f32)
            for n in range(NX - 1):
                s = s + dxb[p, n, j].astype(f32)
            zs2[p, j] = s.astype(bf16).reshape(4, 32, 128)
            for i in range(4):
                off = (2 * i + p + NZ - z) % NZ

                @pl.when(off != 0)
                def _():
                    remote(
                        zs2.at[p, j, i], dzb.at[off - 1, j], dz_s, dz_r.at[off - 1], at_z(off)
                    ).start()

            return 0

        lax.fori_loop(0, DCH, chunk, 0)

    def finish(p):
        @pl.when(z % 2 == p)
        def _():
            for o in range(1, NZ):
                wait_bytes(dzb.at[o - 1], dz_r.at[o - 1])
            for j in range(DCH):
                s = zs2[p, j, z // 2].astype(f32)
                for n in range(NZ - 1):
                    s = s + dzb[n, j].astype(f32)
                s = jnp.concatenate([s[8 * h : 8 * h + 8] for h in range(DCW // 128)], axis=1)
                cols = slice(j * DCW, j * DCW + DCW)
                out[:, cols] = (stream[:, cols] + s).astype(bf16)

    combine(6)
    finish_merge(0)
    combine(7)
    for i in I_ORDER:
        spread(0, i)
    finish_merge(1)
    for i in I_ORDER:
        forward(0, i)
    for i in I_ORDER:
        spread(1, i)
    gathered(0)
    rebuild(0)
    wait_bytes(wgu, w_sem)
    project(0)
    for i in I_ORDER:
        forward(1, i)
    sum_cores(0)
    gathered(1)
    rebuild(1)
    project(1)
    activate(0)
    sum_cores(1)
    hid_forward(0)
    wait_bytes(wdv, d_sem)
    activate(1)
    down(0)
    hid_forward(1)
    sum_x(0)
    down(1)
    sum_x(1)
    finish(0)
    finish(1)

    wait_bytes(sbuf.at[pl.ds(1, 3)], ax_s)
    wait_bytes(zs.at[pl.ds(0, 7)], az_s)
    wait_bytes(ag.at[pl.ds(0, 7)], gz_s)
    wait_bytes(ag.at[pl.ds(0, 24)], gx_s)
    wait_bytes(ssc, sc_s)
    wait_bytes(ssr, ss_s)
    wait_bytes(gs, c_s)
    wait_bytes(yb, y_s)
    wait_bytes(hid.at[0, pl.ds(0, 96)], hy_s)
    wait_bytes(hid.at[0], hc_s)
    wait_bytes(dxb, dx_s)
    wait_bytes(dzb, dz_s)


def body(queries, cache_keys, cache_values, residual, norm_gain, w_gate, w_up, w_down):
    vmem = pl.BlockSpec(memory_space=pltpu.VMEM)
    hbm = pl.BlockSpec(memory_space=pl.ANY)
    dma = pltpu.SemaphoreType.DMA
    shape = jax.ShapeDtypeStruct((OWN, LOCAL), bf16)
    scratch = [
        pltpu.VMEM((HD + 16, CTX), bf16),
        pltpu.VMEM((CTX, COLS), f32),
        pltpu.VMEM((NX, NZ, PIECE, 128), bf16),
        pltpu.VMEM((NX - 1, NZ, PIECE, 128), bf16),
        pltpu.VMEM((NZ, PIECE, 128), bf16),
        pltpu.VMEM((NZ - 1, PIECE, 128), bf16),
        pltpu.VMEM((OWN, LOCAL), f32),
        pltpu.VMEM((NKV, PIECE, 128), bf16),
        pltpu.VMEM((2, 128, LOCAL), bf16),
        pltpu.VMEM((2, 128, 128), f32),
        pltpu.VMEM((2, 64, 128), f32),
        pltpu.VMEM((2, NY - 1, 16, 128), f32),
        pltpu.VMEM((FCH, LOCAL, 256), bf16),
        pltpu.VMEM((DCH, UNITS, DCW), bf16),
        pltpu.VMEM((2, FCH, 128, 256), f32),
        pltpu.VMEM((2, FCH, 64, 256), bf16),
        pltpu.VMEM((2, FCH, 64, 256), bf16),
        pltpu.VMEM((2, FCH, NY, 16, 256), bf16),
        pltpu.VMEM((2, NY - 1, FCH, 16, 256), bf16),
        pltpu.VMEM((2, 128, UNITS), bf16),
        pltpu.VMEM((NKV // 2, DCW // 128, OWN, 128), f32),
        pltpu.VMEM((2, DCH, NX, 128, 128), bf16),
        pltpu.VMEM((2, NX - 1, DCH, 128, 128), bf16),
        pltpu.VMEM((2, DCH, 4, 32, 128), bf16),
        pltpu.VMEM((NZ - 1, DCH, 32, 128), bf16),
        dma, dma,
        dma, dma((NX - 1, NZ)),
        dma, dma((NZ - 1,)),
        dma, dma((NZ - 1,)),
        dma, dma((2, NZ)), dma((2, 2)),
        dma, dma((2,)),
        dma, dma((2, NY - 1)),
        dma, dma((2, FCH)),
        dma, dma((2, NY - 1)),
        dma, dma((2, NY - 1)),
        dma, dma((2,)),
        dma, dma((2, NX - 1, DCH)),
        dma, dma((NZ - 1,)),
    ]
    return pl.pallas_call(
        kernel,
        out_shape=(shape, shape),
        in_specs=[vmem] * 5 + [hbm] * 3,
        out_specs=(vmem, vmem),
        scratch_shapes=scratch,
        name="layer",
        compiler_params=pltpu.CompilerParams(
            collective_id=0, has_side_effects=True, vmem_limit_bytes=56 * 2**20
        ),
    )(
        queries, cache_keys, cache_values, residual, norm_gain.reshape(1, LOCAL), w_gate, w_up, w_down
    )


def solution(mesh):
    in_specs = (
        P(None, "head"),
        P("kv", "head"),
        P("kv", "head"),
        P("kv", "head"),
        P("head"),
        P("head", "kv"),
        P("head", "kv"),
        P("kv", "head"),
    )
    out_specs = (P("kv", "head"), P("kv", "head"))
    return jax.shard_map(body, mesh=mesh, in_specs=in_specs, out_specs=out_specs, check_vma=False)
```

```python
import jax
import jax.numpy as jnp
from jax import lax
from jax.experimental import pallas as pl
from jax.experimental.pallas import tpu as pltpu
from jax.sharding import PartitionSpec as P

MESH = pl.DeviceIdType.MESH
f32, bf16 = jnp.float32, jnp.bfloat16
HD = 128
D = 16384
EPSILON = 1e-05
NX, NZ, NY = 4, 8, 4
NKV = NX * NZ
OWN = 8
CTX = 2560
LOCAL = 2048
UNITS = 896
KC = 256
X_ORDER = (2, 1, 3, 0)
COLS = NX * 128
SCALE = float(HD**-0.5 * 1.4426950408889634)
PIECE = 144
FCH = UNITS // 128
DCH = 4
DCW = LOCAL // DCH
SPLIT = 96
FAR = (4, 5, 3, 6, 2, 7, 1)
I_ORDER = (0, 3, 1, 2)


def split2(v):
    hi = v.astype(bf16).astype(f32)
    return hi, v - hi


def split3(v):
    hi, rest = split2(v)
    mid, low = split2(rest)
    return hi, mid, low


def stats_rows(peak, total):
    width = peak.shape[1]
    rows = [*split3(peak), *split2(total), jnp.zeros((11, width), f32)]
    return jnp.concatenate(rows, axis=0).astype(bf16)


def read_stats(ref):
    s = ref[128:PIECE, :].astype(f32)
    return s[0:1] + s[1:2] + s[2:3], s[3:4] + s[4:5]


def wait_bytes(ref, sem):
    pltpu.make_async_copy(ref, ref, sem).wait()


def kernel(
    q_in, k_in, v_in, res_in, gain_in, wg, wu, wd, outs,
    q, k, v, res, gain, q_sem, k_sem, v_sem, res_sem, gain_sem,
    vt, sc, sbuf, xbuf, zs, zbuf, stream, ag, xn, ssb, ssc, ssr, wgu, wdv,
    gacc, gs, cbuf, ys, yb, hid, dsf, ds, dxb, zs2, dzb, fzb, fzs, fxb,
    w_sem, d_sem, ax_s, ax_r, az_s, az_r, gz_s, gz_r, gx_s, gx_r, hx_s, hx_r, hz_s, hz_r,
    sc_s, sc_r, ss_s, ss_r, c_s, c_r, y_s, y_r, hy_s, hy_r, hc_s, hc_r, dx_s, dx_r, dz_s, dz_r, fz_s, fz_r, fx_s, fx_r,
):
    kv, hd = lax.axis_index("kv"), lax.axis_index("head")
    x, z = kv // NZ, kv % NZ
    y, c = hd // 2, hd % 2

    def at_x(dx):
        return (((x + dx) % NX) * NZ + z, hd)

    def at_z(o):
        return (x * NZ + (z + o) % NZ, hd)

    def at_y(dy):
        return (kv, ((y + dy) % NY) * 2 + c)

    other = (kv, y * 2 + 1 - c)

    def remote(src, dst, send, recv, dev):
        return pltpu.make_async_remote_copy(
            src_ref=src, dst_ref=dst, send_sem=send, recv_sem=recv, device_id=dev, device_id_type=MESH
        )

    loads = [(k_in, k, k_sem), (q_in, q, q_sem), (v_in, v, v_sem), (res_in, res, res_sem), (gain_in, gain, gain_sem)]
    for src, dst, sem in loads:
        pltpu.make_async_copy(src, dst, sem).start()

    barrier = pltpu.get_barrier_semaphore()
    peers = [at_x(o) for o in range(1, NX)] + [at_z(o) for o in range(1, NZ)] + [at_y(o) for o in range(1, NY)] + [other]
    for dev in peers:
        pl.semaphore_signal(barrier, inc=1, device_id=dev, device_id_type=MESH)

    vt[HD:] = jnp.ones((16, CTX), bf16)

    def z_off(j):
        i = j % 4
        same = jnp.where(i == 0, 4, jnp.where(i == 1, 2, jnp.where(i == 2, 6, 0)))
        cross = jnp.where(i == 0, 3, jnp.where(i == 1, 5, jnp.where(i == 2, 1, 7)))
        return jnp.where((z + j // 4) % 2 == 0, same, cross)

    def z_to(j):
        return (z + z_off(j)) % NZ

    def queries_of(j):
        zt = z_to(j)
        tiles = []
        for dx in X_ORDER:
            owner = ((x + dx) % NX) * NZ + zt
            rows = q[pl.ds(pl.multiple_of(owner // 2 * 16, 16), 16), :].astype(f32)
            rows = jnp.where(zt % 2 == 0, rows[:8], rows[8:])
            tiles += [rows[:, 128 * h : 128 * h + 128] for h in range(16)]
        return jnp.concatenate(tiles, axis=0).astype(bf16)

    def scores(i, qb, top):
        rows = pl.ds(i * KC, KC)
        s = lax.dot_general(k[rows, :], qb, (((1,), (1,)), ((), ())), preferred_element_type=f32)
        sc[rows, :] = s
        m = jnp.max(s.reshape(KC // 8, 8, COLS), axis=0)
        return m if top is None else jnp.maximum(top, m)

    def add(a, b):
        return b if a is None else a + b

    def step(j, top):
        qb = queries_of((j + 1) % NZ)
        peak = jnp.max(top, axis=0, keepdims=True) * SCALE
        acc = following = None
        for i in range(CTX // KC):
            rows = pl.ds(i * KC, KC)
            p = jnp.exp2(sc[rows, :] * SCALE - peak)
            acc = add(acc, jnp.dot(vt[:, rows], p.astype(bf16), preferred_element_type=f32))
            following = scores(i, qb, following)
        stats = stats_rows(peak, acc[HD : HD + 1])
        acc = acc[:HD].astype(bf16)
        for n, dx in enumerate(X_ORDER):
            cols = slice(n * 128, n * 128 + 128)
            sbuf[dx, j, :HD, :] = acc[:, cols]
            sbuf[dx, j, HD:PIECE, :] = stats[:, cols]
        for dx in X_ORDER[:3]:
            remote(sbuf.at[dx, j], xbuf.at[dx - 1, j], ax_s, ax_r.at[dx - 1, j], at_x(dx)).start()
        return following

    def merge(refs):
        stats = [read_stats(r) for r in refs]
        peak = stats[0][0]
        for m, _ in stats[1:]:
            peak = jnp.maximum(peak, m)
        factors = [jnp.exp2(m - peak) for m, _ in stats]
        total = None
        for f, (_, t) in zip(factors, stats):
            total = add(total, f * t)
        return peak, total, factors

    def weighted(refs, weights):
        acc = None
        for r, w in zip(refs, weights):
            acc = add(acc, r[:128, :].astype(f32) * w)
        return acc

    def combine(g):
        for dx in range(1, NX):
            remote(sbuf.at[dx, g], xbuf.at[dx - 1, g], ax_s, ax_r.at[dx - 1, g], at_x(dx)).wait_recv()
        refs = [sbuf.at[0, g]] + [xbuf.at[n, g] for n in range(NX - 1)]
        peak, total, factors = merge(refs)
        zs[g, :128, :] = weighted(refs, factors).astype(bf16)
        zs[g, 128:PIECE, :] = stats_rows(peak, total)
        off = z_off(g)

        @pl.when(off != 0)
        def _():
            remote(zs.at[g], zbuf.at[off - 1], az_s, az_r.at[off - 1], at_z(off)).start()

    for src, dst, sem in loads[:2]:
        pltpu.make_async_copy(src, dst, sem).wait()
    first = queries_of(0)
    top = None
    for i in range(CTX // KC):
        top = scores(i, first, top)
    for src, dst, sem in loads[2:]:
        pltpu.make_async_copy(src, dst, sem).wait()
    for j in range(FCH):
        cols = pl.ds(j * 128, 128)
        pltpu.make_async_copy(wg.at[:, cols], wgu.at[j, :, pl.ds(0, 128)], w_sem).start()
        pltpu.make_async_copy(wu.at[:, cols], wgu.at[j, :, pl.ds(128, 128)], w_sem).start()
    for j in range(DCH):
        pltpu.make_async_copy(wd.at[:, pl.ds(j * DCW, DCW)], wdv.at[j], d_sem).start()

    vt[:HD] = v[...].astype(f32).T.astype(bf16)

    pl.semaphore_wait(barrier, len(peers))

    def gather_z(o):
        return remote(part(kv), part(kv), gz_s, gz_r.at[o - 1], at_z(o))

    def part(src):
        return ag.at[src, pl.ds(0, SPLIT)]

    def rest(src):
        return ag.at[src, pl.ds(SPLIT, PIECE - SPLIT)]

    def rest_x(src, dx):
        return remote(rest(src), rest(src), hx_s, hx_r.at[dx - 1], at_x(dx))

    def rest_z(src):
        for o in FAR:
            remote(rest(src), rest(src), hz_s, hz_r.at[o - 1], at_z(o)).start()

    def pass_rest(p):
        @pl.when(z % 2 == p)
        def _():
            rest_z(kv)
            for dx in (1, 3, 2):
                src = ((x + NX - dx) % NX) * NZ + z
                rest_x(src, dx).wait_recv()
                rest_z(src)

    def finish_merge(p):
        @pl.when(z % 2 == p)
        def _():
            for o in range(1, NZ):
                remote(zs.at[0], zbuf.at[o - 1], az_s, az_r.at[o - 1], at_z(o)).wait_recv()
            refs = [zs.at[4 * p + 3]] + [zbuf.at[n] for n in range(NZ - 1)]
            _, total, factors = merge(refs)
            inv = 1.0 / total
            att = weighted(refs, [f * inv for f in factors]).T
            att = jnp.concatenate([att[8 * h : 8 * h + 8, :] for h in range(16)], axis=1).astype(bf16)
            outs[0] = att
            st = res[...].astype(f32) + att.astype(f32)
            stream[...] = st
            squares = jnp.broadcast_to(jnp.sum(st * st, axis=1, keepdims=True), (OWN, 128))
            t = st * gain[...]
            rows = jnp.concatenate([t[:, 128 * h : 128 * h + 128] for h in range(16)], axis=0)
            ag[kv, :128, :] = rows.astype(bf16)
            ag[kv, 128:PIECE, :] = jnp.concatenate(split2(squares), axis=0).astype(bf16)
            for o in FAR:
                gather_z(o).start()
            for dx in (2, 1, 3):
                rest_x(kv, dx).start()

    def attend(j, top):
        top = step(j, top)

        @pl.when(j >= 2)
        def _():
            combine(j - 2)

        @pl.when(j == NZ - 1)
        def _():
            finish_merge(0)

        return top

    lax.fori_loop(0, NZ, attend, top)

    def gather_x(src, dx, recv):
        return remote(part(src), part(src), gx_s, recv, at_x(dx))

    def source(p, i):
        o = 2 * i + (z + p) % 2
        return o, (z + NZ - o) % NZ

    def spread(p, i):
        o, zo = source(p, i)
        src = x * NZ + zo

        @pl.when(o != 0)
        def _():
            remote(part(src), part(src), gz_s, gz_r.at[o - 1], at_z(o)).wait_recv()

        for dx in (2, 1, 3):
            gather_x(src, dx, gx_r.at[dx - 1, o]).start()

    def gathered(p):
        for i in I_ORDER:
            o, zo = source(p, i)
            for dx in range(1, NX):
                gather_x(((x + NX - dx) % NX) * NZ + zo, dx, gx_r.at[dx - 1, o]).wait_recv()

            @pl.when(o != 0)
            def _():
                wait_bytes(ag.at[pl.ds(0, NX), pl.ds(SPLIT, PIECE - SPLIT)], hz_r.at[o - 1])

    def rebuild(p):
        def pair(i, _):
            first = (i // 2) * NZ + 4 * (i % 2) + p
            a = ag[first].astype(f32)
            b = ag[first + 2].astype(f32)
            rows = pl.ds(pl.multiple_of(i * 16, 16), 16)
            for h in range(16):
                tile = jnp.concatenate([a[8 * h : 8 * h + 8], b[8 * h : 8 * h + 8]], axis=0)
                xn[p, rows, 128 * h : 128 * h + 128] = tile.astype(bf16)
            ssb[p, rows, :] = jnp.concatenate([a[128:136] + a[136:144], b[128:136] + b[136:144]], axis=0)
            return 0

        lax.fori_loop(0, 8, pair, 0)

    mine = pl.ds(pl.multiple_of(c * 64, 64), 64)
    theirs = pl.ds(pl.multiple_of((1 - c) * 64, 64), 64)

    def rows_at(yy, cc):
        return pl.ds(pl.multiple_of((cc * NY + yy) * 16, 16), 16)

    own16 = rows_at(y, c)

    def square_core(p):
        return remote(ssb.at[p, theirs], ssc.at[p], sc_s, sc_r.at[p], other)

    def square_y(p, dy):
        src = ssb.at[p, rows_at((y + dy) % NY, c)]
        return remote(src, ssr.at[p, dy - 1], ss_s, ss_r.at[p, dy - 1], at_y(dy))

    def core_copy(p, j):
        return remote(gs.at[p, j], cbuf.at[p, j], c_s, c_r.at[p, j], other)

    def project(p):
        square_core(p).start()

        def chunk(j, _):
            gacc[p, j] = jnp.dot(xn[p], wgu[j], preferred_element_type=f32)
            gs[p, j] = gacc[p, j, theirs, :].astype(bf16)
            core_copy(p, j).start()
            return 0

        lax.fori_loop(0, FCH, chunk, 0)

    def sum_cores(p):
        square_core(p).wait_recv()
        ssb[p, mine, :] = ssb[p, mine, :] + ssc[p]
        for dy in (2, 1, 3):
            square_y(p, dy).start()

        def chunk(j, _):
            core_copy(p, j).wait_recv()
            s = gacc[p, j, mine, :] + cbuf[p, j].astype(f32)
            gacc[p, j, mine, :] = s
            ys[p, j] = s.astype(bf16).reshape(NY, 16, 256)
            for dy in (2, 1, 3):
                to = (y + dy) % NY
                remote(ys.at[p, j, to], yb.at[p, dy - 1, j], y_s, y_r.at[p, dy - 1], at_y(dy)).start()
            return 0

        lax.fori_loop(0, FCH, chunk, 0)

    def hid_rows(p, yy):
        return hid.at[p, rows_at(yy, c)]

    def hid_y(p, yy, dy):
        return remote(hid_rows(p, yy), hid_rows(p, yy), hy_s, hy_r.at[p, dy - 1], at_y(dy))

    def hid_core(p, yy):
        return remote(hid_rows(p, yy), hid_rows(p, yy), hc_s, hc_r.at[p], other)

    def activate(p):
        for dy in range(1, NY):
            square_y(p, dy).wait_recv()
        squares = ssb[p, own16, :]
        for n in range(NY - 1):
            squares = squares + ssr[p, n]
        scale = lax.rsqrt(squares / D + EPSILON)
        for dy in range(1, NY):
            wait_bytes(yb.at[p, dy - 1], y_r.at[p, dy - 1])
        for j in range(FCH):
            s = gacc[p, j, own16, :]
            for n in range(NY - 1):
                s = s + yb[p, n, j].astype(f32)
            gate = s[:, :128] * scale
            up = s[:, 128:] * scale
            hid[p, own16, 128 * j : 128 * j + 128] = (gate / (1.0 + jnp.exp(-gate)) * up).astype(bf16)
        for dy in (2, 1, 3):
            hid_y(p, y, dy).start()
        hid_core(p, y).start()

    def hid_forward(p):
        for dy in (1, 3, 2):
            yy = (y + NY - dy) % NY
            hid_y(p, yy, dy).wait_recv()
            hid_core(p, yy).start()

    def down_x(p, j, dx):
        src = ds.at[p, j, (x + dx) % NX]
        return remote(src, dxb.at[p, dx - 1, j], dx_s, dx_r.at[p, dx - 1, j], at_x(dx))

    def down(p):
        wait_bytes(hid.at[p, theirs], hc_r.at[p])

        def chunk(j):
            acc = jnp.dot(hid[p], wdv[j], preferred_element_type=f32)
            for h in range(DCW // 128):
                dsf[:, h] = acc[:, 128 * h : 128 * h + 128].reshape(NKV // 2, OWN, 128)
            ds[p, j] = dsf[...].reshape(NX, 128, 128).astype(bf16)

        chunk(0)
        for n in range(4):
            off, i = owner_of(p, n)

            @pl.when(off != 0)
            def _():
                src = ds.at[p, 0, :, pl.ds(pl.multiple_of(32 * i, 32), 32)]
                remote(src, fzb.at[off - 1], fz_s, fz_r.at[off - 1], at_z(off)).start()

        def later(j, _):
            chunk(j)
            for dx in (2, 1, 3):
                down_x(p, j, dx).start()
            return 0

        lax.fori_loop(1, DCH, later, 0)

    def owner_of(p, n):
        off = z_off(4 * p + n)
        return off, ((z + off) % NZ) // 2

    def sum_z(p):
        @pl.when(z % 2 == p)
        def _():
            for o in range(1, NZ):
                remote(fzb.at[o - 1], fzb.at[o - 1], fz_s, fz_r.at[o - 1], at_z(o)).wait_recv()
            s = ds[p, 0, :, pl.ds(pl.multiple_of(z // 2 * 32, 32), 32), :].astype(f32)
            for n in range(NZ - 1):
                s = s + fzb[n].astype(f32)
            fzs[...] = s.astype(bf16)
            for dx in (2, 1, 3):
                last_x(dx).start()

    def last_x(dx):
        return remote(fzs.at[(x + dx) % NX], fxb.at[dx - 1], fx_s, fx_r.at[dx - 1], at_x(dx))

    def sum_x(p):
        def chunk(j, _):
            for dx in range(1, NX):
                down_x(p, j, dx).wait_recv()
            s = ds[p, j, x].astype(f32)
            for n in range(NX - 1):
                s = s + dxb[p, n, j].astype(f32)
            zs2[p, j] = s.astype(bf16).reshape(4, 32, 128)
            for n in range(4):
                off, i = owner_of(p, n)

                @pl.when(off != 0)
                def _():
                    remote(
                        zs2.at[p, j, i], dzb.at[off - 1, j - 1], dz_s, dz_r.at[off - 1], at_z(off)
                    ).start()

            return 0

        lax.fori_loop(1, DCH, chunk, 0)

    def finish(p):
        @pl.when(z % 2 == p)
        def _():
            for dx in range(1, NX):
                last_x(dx).wait_recv()
            for o in range(1, NZ):
                wait_bytes(dzb.at[o - 1], dz_r.at[o - 1])
            for j in range(DCH):
                if j == 0:
                    s = fzs[x].astype(f32)
                    for n in range(NX - 1):
                        s = s + fxb[n].astype(f32)
                else:
                    s = zs2[p, j, z // 2].astype(f32)
                    for n in range(NZ - 1):
                        s = s + dzb[n, j - 1].astype(f32)
                s = jnp.concatenate([s[8 * h : 8 * h + 8] for h in range(DCW // 128)], axis=1)
                cols = slice(j * DCW, j * DCW + DCW)
                outs[1, :, cols] = (stream[:, cols] + s).astype(bf16)

    combine(6)
    combine(7)
    finish_merge(1)
    for i in I_ORDER:
        spread(0, i)
    pass_rest(0)
    pass_rest(1)
    for i in I_ORDER:
        spread(1, i)
    gathered(0)
    rebuild(0)
    wait_bytes(wgu, w_sem)
    project(0)
    sum_cores(0)
    gathered(1)
    rebuild(1)
    project(1)
    activate(0)
    sum_cores(1)
    hid_forward(0)
    wait_bytes(wdv, d_sem)
    activate(1)
    down(0)
    hid_forward(1)
    down(1)
    sum_z(0)
    sum_x(0)
    sum_x(1)
    sum_z(1)
    finish(0)
    finish(1)

    wait_bytes(sbuf.at[pl.ds(1, 3)], ax_s)
    wait_bytes(zs.at[pl.ds(0, 7)], az_s)
    wait_bytes(ag.at[pl.ds(0, 7), pl.ds(0, SPLIT)], gz_s)
    wait_bytes(ag.at[pl.ds(0, 24), pl.ds(0, SPLIT)], gx_s)
    wait_bytes(ag.at[pl.ds(0, 3), pl.ds(SPLIT, PIECE - SPLIT)], hx_s)
    wait_bytes(ag.at[pl.ds(0, 28), pl.ds(SPLIT, PIECE - SPLIT)], hz_s)
    wait_bytes(ssc, sc_s)
    wait_bytes(ssr, ss_s)
    wait_bytes(gs, c_s)
    wait_bytes(yb, y_s)
    wait_bytes(hid.at[0, pl.ds(0, 96)], hy_s)
    wait_bytes(hid.at[0], hc_s)
    wait_bytes(dxb.at[:, :, pl.ds(1, DCH - 1)], dx_s)
    wait_bytes(fzb, fz_s)
    wait_bytes(fxb, fx_s)
    wait_bytes(dzb, dz_s)


def body(queries, cache_keys, cache_values, residual, norm_gain, w_gate, w_up, w_down):
    vmem = pl.BlockSpec(memory_space=pltpu.VMEM)
    hbm = pl.BlockSpec(memory_space=pl.ANY)
    dma = pltpu.SemaphoreType.DMA
    shape = pltpu.VMEM((2, OWN, LOCAL), bf16)
    scratch = [
        pltpu.VMEM((256, LOCAL), bf16),
        pltpu.VMEM((CTX, HD), bf16),
        pltpu.VMEM((CTX, HD), bf16),
        pltpu.VMEM((OWN, LOCAL), bf16),
        pltpu.VMEM((1, LOCAL), f32),
        dma, dma, dma, dma, dma,
        pltpu.VMEM((HD + 16, CTX), bf16),
        pltpu.VMEM((CTX, COLS), f32),
        pltpu.VMEM((NX, NZ, PIECE, 128), bf16),
        pltpu.VMEM((NX - 1, NZ, PIECE, 128), bf16),
        pltpu.VMEM((NZ, PIECE, 128), bf16),
        pltpu.VMEM((NZ - 1, PIECE, 128), bf16),
        pltpu.VMEM((OWN, LOCAL), f32),
        pltpu.VMEM((NKV, PIECE, 128), bf16),
        pltpu.VMEM((2, 128, LOCAL), bf16),
        pltpu.VMEM((2, 128, 128), f32),
        pltpu.VMEM((2, 64, 128), f32),
        pltpu.VMEM((2, NY - 1, 16, 128), f32),
        pltpu.VMEM((FCH, LOCAL, 256), bf16),
        pltpu.VMEM((DCH, UNITS, DCW), bf16),
        pltpu.VMEM((2, FCH, 128, 256), f32),
        pltpu.VMEM((2, FCH, 64, 256), bf16),
        pltpu.VMEM((2, FCH, 64, 256), bf16),
        pltpu.VMEM((2, FCH, NY, 16, 256), bf16),
        pltpu.VMEM((2, NY - 1, FCH, 16, 256), bf16),
        pltpu.VMEM((2, 128, UNITS), bf16),
        pltpu.VMEM((NKV // 2, DCW // 128, OWN, 128), f32),
        pltpu.VMEM((2, DCH, NX, 128, 128), bf16),
        pltpu.VMEM((2, NX - 1, DCH, 128, 128), bf16),
        pltpu.VMEM((2, DCH, 4, 32, 128), bf16),
        pltpu.VMEM((NZ - 1, DCH - 1, 32, 128), bf16),
        pltpu.VMEM((NZ - 1, NX, 32, 128), bf16),
        pltpu.VMEM((NX, 32, 128), bf16),
        pltpu.VMEM((NX - 1, 32, 128), bf16),
        dma, dma,
        dma, dma((NX - 1, NZ)),
        dma, dma((NZ - 1,)),
        dma, dma((NZ - 1,)),
        dma, dma((NX - 1, NZ)),
        dma, dma((NX - 1,)),
        dma, dma((NZ - 1,)),
        dma, dma((2,)),
        dma, dma((2, NY - 1)),
        dma, dma((2, FCH)),
        dma, dma((2, NY - 1)),
        dma, dma((2, NY - 1)),
        dma, dma((2,)),
        dma, dma((2, NX - 1, DCH)),
        dma, dma((NZ - 1,)),
        dma, dma((NZ - 1,)),
        dma, dma((NX - 1,)),
    ]
    outs = pl.pallas_call(
        kernel,
        out_shape=shape,
        in_specs=[hbm] * 8,
        out_specs=vmem,
        scratch_shapes=scratch,
        name="layer",
        compiler_params=pltpu.CompilerParams(
            collective_id=0, has_side_effects=True, vmem_limit_bytes=56 * 2**20
        ),
    )(
        queries, cache_keys, cache_values, residual, norm_gain.reshape(1, LOCAL), w_gate, w_up, w_down
    )
    return outs[0], outs[1]


def solution(mesh):
    in_specs = (
        P(None, "head"),
        P("kv", "head"),
        P("kv", "head"),
        P("kv", "head"),
        P("head"),
        P("head", "kv"),
        P("head", "kv"),
        P("kv", "head"),
    )
    out_specs = (P("kv", "head"), P("kv", "head"))
    return jax.shard_map(body, mesh=mesh, in_specs=in_specs, out_specs=out_specs, check_vma=False)
```

```python
import jax
import jax.numpy as jnp
from jax import lax
from jax.experimental import pallas as pl
from jax.experimental.pallas import tpu as pltpu
from jax.sharding import PartitionSpec as P

MESH = pl.DeviceIdType.MESH
f32, bf16 = jnp.float32, jnp.bfloat16
HD = 128
D = 16384
EPSILON = 1e-05
NX, NZ, NY = 4, 8, 4
NKV = NX * NZ
OWN = 8
CTX = 2560
LOCAL = 2048
UNITS = 896
KC = 256
X_ORDER = (2, 1, 3, 0)
COLS = NX * 128
SCALE = float(HD**-0.5 * 1.4426950408889634)
PIECE = 144
FCH = UNITS // 128
DCH = 4
DCW = LOCAL // DCH
SPLIT = 96
FAR = (4, 5, 3, 6, 2, 7, 1)
I_ORDER = (0, 3, 1, 2)


def split2(v):
    hi = v.astype(bf16).astype(f32)
    return hi, v - hi


def split3(v):
    hi, rest = split2(v)
    mid, low = split2(rest)
    return hi, mid, low


def stats_rows(peak, total):
    width = peak.shape[1]
    rows = [*split3(peak), *split2(total), jnp.zeros((11, width), f32)]
    return jnp.concatenate(rows, axis=0).astype(bf16)


def read_stats(ref):
    s = ref[128:PIECE, :].astype(f32)
    return s[0:1] + s[1:2] + s[2:3], s[3:4] + s[4:5]


def wait_bytes(ref, sem):
    pltpu.make_async_copy(ref, ref, sem).wait()


def kernel(
    q_in, k_in, v_in, res_in, gain_in, wg, wu, wd, outs,
    q, k, v, res, gain, q_sem, k_sem, v_sem, res_sem, gain_sem,
    vt, sc, sbuf, xbuf, zs, zbuf, stream, ag, ginv, xn, ssb, ssc, ssr, wgu, wdv,
    gacc, gs, cbuf, ys, yb, hid, dsf, ds, dxb, zs2, dzb, fzb, fzs, fxb,
    w_sem, d_sem, ax_s, ax_r, az_s, az_r, gz_s, gz_r, gx_s, gx_r, hx_s, hx_r, hz_s, hz_r,
    sc_s, sc_r, ss_s, ss_r, c_s, c_r, y_s, y_r, hy_s, hy_r, hc_s, hc_r, dx_s, dx_r, dz_s, dz_r, fz_s, fz_r, fx_s, fx_r,
):
    kv, hd = lax.axis_index("kv"), lax.axis_index("head")
    x, z = kv // NZ, kv % NZ
    y, c = hd // 2, hd % 2

    def at_x(dx):
        return (((x + dx) % NX) * NZ + z, hd)

    def at_z(o):
        return (x * NZ + (z + o) % NZ, hd)

    def at_y(dy):
        return (kv, ((y + dy) % NY) * 2 + c)

    other = (kv, y * 2 + 1 - c)

    def remote(src, dst, send, recv, dev):
        return pltpu.make_async_remote_copy(
            src_ref=src, dst_ref=dst, send_sem=send, recv_sem=recv, device_id=dev, device_id_type=MESH
        )

    loads = [(k_in, k, k_sem), (q_in, q, q_sem), (v_in, v, v_sem), (res_in, res, res_sem), (gain_in, gain, gain_sem)]
    for src, dst, sem in loads:
        pltpu.make_async_copy(src, dst, sem).start()

    barrier = pltpu.get_barrier_semaphore()
    peers = [at_x(o) for o in range(1, NX)] + [at_z(o) for o in range(1, NZ)] + [at_y(o) for o in range(1, NY)] + [other]
    for dev in peers:
        pl.semaphore_signal(barrier, inc=1, device_id=dev, device_id_type=MESH)

    vt[HD:] = jnp.ones((16, CTX), bf16)

    def z_off(j):
        i = j % 4
        same = jnp.where(i == 0, 4, jnp.where(i == 1, 2, jnp.where(i == 2, 6, 0)))
        cross = jnp.where(i == 0, 3, jnp.where(i == 1, 5, jnp.where(i == 2, 1, 7)))
        return jnp.where((z + j // 4) % 2 == 0, same, cross)

    def z_to(j):
        return (z + z_off(j)) % NZ

    def queries_of(j):
        zt = z_to(j)
        tiles = []
        for dx in X_ORDER:
            owner = ((x + dx) % NX) * NZ + zt
            rows = q[pl.ds(pl.multiple_of(owner // 2 * 16, 16), 16), :].astype(f32)
            rows = jnp.where(zt % 2 == 0, rows[:8], rows[8:])
            tiles += [rows[:, 128 * h : 128 * h + 128] for h in range(16)]
        return jnp.concatenate(tiles, axis=0).astype(bf16)

    def scores(i, qb, top):
        rows = pl.ds(i * KC, KC)
        s = lax.dot_general(k[rows, :], qb, (((1,), (1,)), ((), ())), preferred_element_type=f32)
        sc[rows, :] = s
        m = jnp.max(s.reshape(KC // 8, 8, COLS), axis=0)
        return m if top is None else jnp.maximum(top, m)

    def add(a, b):
        return b if a is None else a + b

    def step(j, top):
        qb = queries_of((j + 1) % NZ)
        peak = jnp.max(top, axis=0, keepdims=True) * SCALE
        acc = following = None
        for i in range(CTX // KC):
            rows = pl.ds(i * KC, KC)
            p = jnp.exp2(sc[rows, :] * SCALE - peak)
            acc = add(acc, jnp.dot(vt[:, rows], p.astype(bf16), preferred_element_type=f32))
            following = scores(i, qb, following)
        stats = stats_rows(peak, acc[HD : HD + 1])
        acc = acc[:HD].astype(bf16)
        for n, dx in enumerate(X_ORDER):
            cols = slice(n * 128, n * 128 + 128)
            sbuf[dx, j, :HD, :] = acc[:, cols]
            sbuf[dx, j, HD:PIECE, :] = stats[:, cols]
        for dx in X_ORDER[:3]:
            remote(sbuf.at[dx, j], xbuf.at[dx - 1, j], ax_s, ax_r.at[dx - 1, j], at_x(dx)).start()
        return following

    def merge(refs):
        stats = [read_stats(r) for r in refs]
        peak = stats[0][0]
        for m, _ in stats[1:]:
            peak = jnp.maximum(peak, m)
        factors = [jnp.exp2(m - peak) for m, _ in stats]
        total = None
        for f, (_, t) in zip(factors, stats):
            total = add(total, f * t)
        return peak, total, factors

    def weighted(refs, weights):
        acc = None
        for r, w in zip(refs, weights):
            acc = add(acc, r[:128, :].astype(f32) * w)
        return acc

    def combine(g):
        for dx in range(1, NX):
            remote(sbuf.at[dx, g], xbuf.at[dx - 1, g], ax_s, ax_r.at[dx - 1, g], at_x(dx)).wait_recv()
        refs = [sbuf.at[0, g]] + [xbuf.at[n, g] for n in range(NX - 1)]
        peak, total, factors = merge(refs)
        zs[g, :128, :] = weighted(refs, factors).astype(bf16)
        zs[g, 128:PIECE, :] = stats_rows(peak, total)
        off = z_off(g)

        @pl.when(off != 0)
        def _():
            remote(zs.at[g], zbuf.at[off - 1], az_s, az_r.at[off - 1], at_z(off)).start()

    for src, dst, sem in loads[:2]:
        pltpu.make_async_copy(src, dst, sem).wait()
    first = queries_of(0)
    top = None
    for i in range(CTX // KC):
        top = scores(i, first, top)
    for src, dst, sem in loads[2:]:
        pltpu.make_async_copy(src, dst, sem).wait()
    for j in range(FCH):
        cols = pl.ds(j * 128, 128)
        pltpu.make_async_copy(wg.at[:, cols], wgu.at[j, :, pl.ds(0, 128)], w_sem).start()
        pltpu.make_async_copy(wu.at[:, cols], wgu.at[j, :, pl.ds(128, 128)], w_sem).start()
    for j in range(DCH):
        pltpu.make_async_copy(wd.at[:, pl.ds(j * DCW, DCW)], wdv.at[j], d_sem).start()

    vt[:HD] = v[...].astype(f32).T.astype(bf16)

    pl.semaphore_wait(barrier, len(peers))

    def gather_z(o):
        return remote(part(kv), part(kv), gz_s, gz_r.at[o - 1], at_z(o))

    def part(src):
        return ag.at[src, pl.ds(0, SPLIT)]

    def rest(src):
        return ag.at[src, pl.ds(SPLIT, 128 - SPLIT)]

    def rest_x(src, dx):
        return remote(rest(src), rest(src), hx_s, hx_r.at[dx - 1], at_x(dx))

    def rest_z(src):
        for o in FAR:
            remote(rest(src), rest(src), hz_s, hz_r.at[o - 1], at_z(o)).start()

    def pass_rest(p):
        @pl.when(z % 2 == p)
        def _():
            rest_z(kv)
            for dx in (1, 3, 2):
                src = ((x + NX - dx) % NX) * NZ + z
                rest_x(src, dx).wait_recv()
                rest_z(src)

    def finish_merge(p):
        @pl.when(z % 2 == p)
        def _():
            for o in range(1, NZ):
                remote(zs.at[0], zbuf.at[o - 1], az_s, az_r.at[o - 1], at_z(o)).wait_recv()
            refs = [zs.at[4 * p + 3]] + [zbuf.at[n] for n in range(NZ - 1)]
            _, total, factors = merge(refs)
            inv = 1.0 / total
            att = weighted(refs, [f * inv for f in factors]).T
            att = jnp.concatenate([att[8 * h : 8 * h + 8, :] for h in range(16)], axis=1).astype(bf16)
            outs[0] = att
            st = res[...].astype(f32) + att.astype(f32)
            stream[...] = st
            t = st * gain[...]
            rows = jnp.concatenate([t[:, 128 * h : 128 * h + 128] for h in range(16)], axis=0)
            ag[kv] = rows.astype(bf16)
            for o in FAR:
                gather_z(o).start()
            for dx in (2, 1, 3):
                rest_x(kv, dx).start()

    def attend(j, top):
        top = step(j, top)

        @pl.when(j >= 3)
        def _():
            combine(j - 3)

        return top

    lax.fori_loop(0, NZ, attend, top)

    def gather_x(src, dx, recv):
        return remote(part(src), part(src), gx_s, recv, at_x(dx))

    def source(p, i):
        o = 2 * i + (z + p) % 2
        return o, (z + NZ - o) % NZ

    def spread(p, i):
        o, zo = source(p, i)
        src = x * NZ + zo

        @pl.when(o != 0)
        def _():
            remote(part(src), part(src), gz_s, gz_r.at[o - 1], at_z(o)).wait_recv()

        for dx in (2, 1, 3):
            gather_x(src, dx, gx_r.at[dx - 1, o]).start()

    def gathered(p):
        for i in I_ORDER:
            o, zo = source(p, i)
            for dx in range(1, NX):
                gather_x(((x + NX - dx) % NX) * NZ + zo, dx, gx_r.at[dx - 1, o]).wait_recv()

            @pl.when(o != 0)
            def _():
                wait_bytes(ag.at[pl.ds(0, NX), pl.ds(SPLIT, 128 - SPLIT)], hz_r.at[o - 1])

    def row_squares(rows):
        st = rows * ginv[...]
        return jnp.sum((st * st).reshape(16, OWN, 128), axis=0)

    def rebuild(p):
        def pair(i, _):
            first = (i // 2) * NZ + 4 * (i % 2) + p
            a = ag[first].astype(f32)
            b = ag[first + 2].astype(f32)
            rows = pl.ds(pl.multiple_of(i * 16, 16), 16)
            for h in range(16):
                tile = jnp.concatenate([a[8 * h : 8 * h + 8], b[8 * h : 8 * h + 8]], axis=0)
                xn[p, rows, 128 * h : 128 * h + 128] = tile.astype(bf16)
            ssb[p, rows, :] = jnp.concatenate([row_squares(a), row_squares(b)], axis=0)
            return 0

        lax.fori_loop(0, 8, pair, 0)

    mine = pl.ds(pl.multiple_of(c * 64, 64), 64)
    theirs = pl.ds(pl.multiple_of((1 - c) * 64, 64), 64)

    def rows_at(yy, cc):
        return pl.ds(pl.multiple_of((cc * NY + yy) * 16, 16), 16)

    own16 = rows_at(y, c)

    def square_core(p):
        return remote(ssb.at[p, theirs], ssc.at[p], sc_s, sc_r.at[p], other)

    def square_y(p, dy):
        src = ssb.at[p, rows_at((y + dy) % NY, c)]
        return remote(src, ssr.at[p, dy - 1], ss_s, ss_r.at[p, dy - 1], at_y(dy))

    def core_copy(p, j):
        return remote(gs.at[p, j], cbuf.at[p, j], c_s, c_r.at[p, j], other)

    def project(p):
        square_core(p).start()

        def chunk(j, _):
            gacc[p, j] = jnp.dot(xn[p], wgu[j], preferred_element_type=f32)
            gs[p, j] = gacc[p, j, theirs, :].astype(bf16)
            core_copy(p, j).start()
            return 0

        lax.fori_loop(0, FCH, chunk, 0)

    def sum_cores(p):
        square_core(p).wait_recv()
        ssb[p, mine, :] = ssb[p, mine, :] + ssc[p]
        for dy in (2, 1, 3):
            square_y(p, dy).start()

        def chunk(j, _):
            core_copy(p, j).wait_recv()
            s = gacc[p, j, mine, :] + cbuf[p, j].astype(f32)
            gacc[p, j, mine, :] = s
            ys[p, j] = s.astype(bf16).reshape(NY, 16, 256)
            for dy in (2, 1, 3):
                to = (y + dy) % NY
                remote(ys.at[p, j, to], yb.at[p, dy - 1, j], y_s, y_r.at[p, dy - 1], at_y(dy)).start()
            return 0

        lax.fori_loop(0, FCH, chunk, 0)

    def hid_rows(p, yy):
        return hid.at[p, rows_at(yy, c)]

    def hid_y(p, yy, dy):
        return remote(hid_rows(p, yy), hid_rows(p, yy), hy_s, hy_r.at[p, dy - 1], at_y(dy))

    def hid_core(p, yy):
        return remote(hid_rows(p, yy), hid_rows(p, yy), hc_s, hc_r.at[p], other)

    def activate(p):
        for dy in range(1, NY):
            square_y(p, dy).wait_recv()
        squares = ssb[p, own16, :]
        for n in range(NY - 1):
            squares = squares + ssr[p, n]
        scale = lax.rsqrt(jnp.sum(squares, axis=1, keepdims=True) / D + EPSILON)
        for dy in range(1, NY):
            wait_bytes(yb.at[p, dy - 1], y_r.at[p, dy - 1])
        for j in range(FCH):
            s = gacc[p, j, own16, :]
            for n in range(NY - 1):
                s = s + yb[p, n, j].astype(f32)
            gate = s[:, :128] * scale
            up = s[:, 128:] * scale
            hid[p, own16, 128 * j : 128 * j + 128] = (gate / (1.0 + jnp.exp(-gate)) * up).astype(bf16)
        for dy in (2, 1, 3):
            hid_y(p, y, dy).start()
        hid_core(p, y).start()

    def hid_forward(p):
        for dy in (1, 3, 2):
            yy = (y + NY - dy) % NY
            hid_y(p, yy, dy).wait_recv()
            hid_core(p, yy).start()

    def down_x(p, j, dx):
        src = ds.at[p, j, (x + dx) % NX]
        return remote(src, dxb.at[p, dx - 1, j], dx_s, dx_r.at[p, dx - 1, j], at_x(dx))

    def down(p):
        wait_bytes(hid.at[p, theirs], hc_r.at[p])

        def chunk(j):
            acc = jnp.dot(hid[p], wdv[j], preferred_element_type=f32)
            for h in range(DCW // 128):
                dsf[:, h] = acc[:, 128 * h : 128 * h + 128].reshape(NKV // 2, OWN, 128)
            ds[p, j] = dsf[...].reshape(NX, 128, 128).astype(bf16)

        chunk(0)
        for n in range(4):
            off, i = owner_of(p, n)

            @pl.when(off != 0)
            def _():
                src = ds.at[p, 0, :, pl.ds(pl.multiple_of(32 * i, 32), 32)]
                remote(src, fzb.at[off - 1], fz_s, fz_r.at[off - 1], at_z(off)).start()

        def later(j, _):
            chunk(j)
            for dx in (2, 1, 3):
                down_x(p, j, dx).start()
            return 0

        lax.fori_loop(1, DCH, later, 0)

    def owner_of(p, n):
        off = z_off(4 * p + n)
        return off, ((z + off) % NZ) // 2

    def sum_z(p):
        @pl.when(z % 2 == p)
        def _():
            for o in range(1, NZ):
                remote(fzb.at[o - 1], fzb.at[o - 1], fz_s, fz_r.at[o - 1], at_z(o)).wait_recv()
            s = ds[p, 0, :, pl.ds(pl.multiple_of(z // 2 * 32, 32), 32), :].astype(f32)
            for n in range(NZ - 1):
                s = s + fzb[n].astype(f32)
            fzs[...] = s.astype(bf16)
            for dx in (2, 1, 3):
                last_x(dx).start()

    def last_x(dx):
        return remote(fzs.at[(x + dx) % NX], fxb.at[dx - 1], fx_s, fx_r.at[dx - 1], at_x(dx))

    def sum_x(p):
        def chunk(j, _):
            for dx in range(1, NX):
                down_x(p, j, dx).wait_recv()
            s = ds[p, j, x].astype(f32)
            for n in range(NX - 1):
                s = s + dxb[p, n, j].astype(f32)
            zs2[p, j] = s.astype(bf16).reshape(4, 32, 128)
            for n in range(4):
                off, i = owner_of(p, n)

                @pl.when(off != 0)
                def _():
                    remote(
                        zs2.at[p, j, i], dzb.at[off - 1, j - 1], dz_s, dz_r.at[off - 1], at_z(off)
                    ).start()

            return 0

        lax.fori_loop(1, DCH, chunk, 0)

    def finish(p):
        @pl.when(z % 2 == p)
        def _():
            for dx in range(1, NX):
                last_x(dx).wait_recv()
            for o in range(1, NZ):
                wait_bytes(dzb.at[o - 1], dz_r.at[o - 1])
            for j in range(DCH):
                if j == 0:
                    s = fzs[x].astype(f32)
                    for n in range(NX - 1):
                        s = s + fxb[n].astype(f32)
                else:
                    s = zs2[p, j, z // 2].astype(f32)
                    for n in range(NZ - 1):
                        s = s + dzb[n, j - 1].astype(f32)
                s = jnp.concatenate([s[8 * h : 8 * h + 8] for h in range(DCW // 128)], axis=1)
                cols = slice(j * DCW, j * DCW + DCW)
                outs[1, :, cols] = (stream[:, cols] + s).astype(bf16)

    finish_merge(0)
    combine(5)
    combine(6)
    combine(7)
    finish_merge(1)
    for i in I_ORDER:
        spread(0, i)
    pass_rest(0)
    pass_rest(1)
    for i in I_ORDER:
        spread(1, i)
    inverse = jnp.broadcast_to(1.0 / gain[...], (OWN, LOCAL))
    ginv[...] = jnp.concatenate([inverse[:, 128 * h : 128 * h + 128] for h in range(16)], axis=0)
    gathered(0)
    rebuild(0)
    wait_bytes(wgu, w_sem)
    project(0)
    sum_cores(0)
    gathered(1)
    rebuild(1)
    project(1)
    activate(0)
    sum_cores(1)
    hid_forward(0)
    wait_bytes(wdv, d_sem)
    activate(1)
    down(0)
    hid_forward(1)
    down(1)
    sum_z(0)
    sum_x(0)
    sum_x(1)
    sum_z(1)
    finish(0)
    finish(1)

    wait_bytes(sbuf.at[pl.ds(1, 3)], ax_s)
    wait_bytes(zs.at[pl.ds(0, 7)], az_s)
    wait_bytes(ag.at[pl.ds(0, 7), pl.ds(0, SPLIT)], gz_s)
    wait_bytes(ag.at[pl.ds(0, 24), pl.ds(0, SPLIT)], gx_s)
    wait_bytes(ag.at[pl.ds(0, 3), pl.ds(SPLIT, 128 - SPLIT)], hx_s)
    wait_bytes(ag.at[pl.ds(0, 28), pl.ds(SPLIT, 128 - SPLIT)], hz_s)
    wait_bytes(ssc, sc_s)
    wait_bytes(ssr, ss_s)
    wait_bytes(gs, c_s)
    wait_bytes(yb, y_s)
    wait_bytes(hid.at[0, pl.ds(0, 96)], hy_s)
    wait_bytes(hid.at[0], hc_s)
    wait_bytes(dxb.at[:, :, pl.ds(1, DCH - 1)], dx_s)
    wait_bytes(fzb, fz_s)
    wait_bytes(fxb, fx_s)
    wait_bytes(dzb, dz_s)


def body(queries, cache_keys, cache_values, residual, norm_gain, w_gate, w_up, w_down):
    vmem = pl.BlockSpec(memory_space=pltpu.VMEM)
    hbm = pl.BlockSpec(memory_space=pl.ANY)
    dma = pltpu.SemaphoreType.DMA
    shape = pltpu.VMEM((2, OWN, LOCAL), bf16)
    scratch = [
        pltpu.VMEM((256, LOCAL), bf16),
        pltpu.VMEM((CTX, HD), bf16),
        pltpu.VMEM((CTX, HD), bf16),
        pltpu.VMEM((OWN, LOCAL), bf16),
        pltpu.VMEM((1, LOCAL), f32),
        dma, dma, dma, dma, dma,
        pltpu.VMEM((HD + 16, CTX), bf16),
        pltpu.VMEM((CTX, COLS), f32),
        pltpu.VMEM((NX, NZ, PIECE, 128), bf16),
        pltpu.VMEM((NX - 1, NZ, PIECE, 128), bf16),
        pltpu.VMEM((NZ, PIECE, 128), bf16),
        pltpu.VMEM((NZ - 1, PIECE, 128), bf16),
        pltpu.VMEM((OWN, LOCAL), f32),
        pltpu.VMEM((NKV, 128, 128), bf16),
        pltpu.VMEM((128, 128), f32),
        pltpu.VMEM((2, 128, LOCAL), bf16),
        pltpu.VMEM((2, 128, 128), f32),
        pltpu.VMEM((2, 64, 128), f32),
        pltpu.VMEM((2, NY - 1, 16, 128), f32),
        pltpu.VMEM((FCH, LOCAL, 256), bf16),
        pltpu.VMEM((DCH, UNITS, DCW), bf16),
        pltpu.VMEM((2, FCH, 128, 256), f32),
        pltpu.VMEM((2, FCH, 64, 256), bf16),
        pltpu.VMEM((2, FCH, 64, 256), bf16),
        pltpu.VMEM((2, FCH, NY, 16, 256), bf16),
        pltpu.VMEM((2, NY - 1, FCH, 16, 256), bf16),
        pltpu.VMEM((2, 128, UNITS), bf16),
        pltpu.VMEM((NKV // 2, DCW // 128, OWN, 128), f32),
        pltpu.VMEM((2, DCH, NX, 128, 128), bf16),
        pltpu.VMEM((2, NX - 1, DCH, 128, 128), bf16),
        pltpu.VMEM((2, DCH, 4, 32, 128), bf16),
        pltpu.VMEM((NZ - 1, DCH - 1, 32, 128), bf16),
        pltpu.VMEM((NZ - 1, NX, 32, 128), bf16),
        pltpu.VMEM((NX, 32, 128), bf16),
        pltpu.VMEM((NX - 1, 32, 128), bf16),
        dma, dma,
        dma, dma((NX - 1, NZ)),
        dma, dma((NZ - 1,)),
        dma, dma((NZ - 1,)),
        dma, dma((NX - 1, NZ)),
        dma, dma((NX - 1,)),
        dma, dma((NZ - 1,)),
        dma, dma((2,)),
        dma, dma((2, NY - 1)),
        dma, dma((2, FCH)),
        dma, dma((2, NY - 1)),
        dma, dma((2, NY - 1)),
        dma, dma((2,)),
        dma, dma((2, NX - 1, DCH)),
        dma, dma((NZ - 1,)),
        dma, dma((NZ - 1,)),
        dma, dma((NX - 1,)),
    ]
    outs = pl.pallas_call(
        kernel,
        out_shape=shape,
        in_specs=[hbm] * 8,
        out_specs=vmem,
        scratch_shapes=scratch,
        name="layer",
        compiler_params=pltpu.CompilerParams(
            collective_id=0, has_side_effects=True, vmem_limit_bytes=56 * 2**20
        ),
    )(
        queries, cache_keys, cache_values, residual, norm_gain.reshape(1, LOCAL), w_gate, w_up, w_down
    )
    return outs[0], outs[1]


def solution(mesh):
    in_specs = (
        P(None, "head"),
        P("kv", "head"),
        P("kv", "head"),
        P("kv", "head"),
        P("head"),
        P("head", "kv"),
        P("head", "kv"),
        P("kv", "head"),
    )
    out_specs = (P("kv", "head"), P("kv", "head"))
    return jax.shard_map(body, mesh=mesh, in_specs=in_specs, out_specs=out_specs, check_vma=False)
```

```python
import jax
import jax.numpy as jnp
from jax import lax
from jax.experimental import pallas as pl
from jax.experimental.pallas import tpu as pltpu
from jax.sharding import PartitionSpec as P

MESH = pl.DeviceIdType.MESH
f32, bf16 = jnp.float32, jnp.bfloat16
HD = 128
D = 16384
EPSILON = 1e-05
NX, NZ, NY = 4, 8, 4
NKV = NX * NZ
OWN = 8
CTX = 2560
LOCAL = 2048
UNITS = 896
KC = 256
X_ORDER = (2, 1, 3, 0)
COLS = NX * 128
SCALE = float(HD**-0.5 * 1.4426950408889634)
PIECE = 144
FCH = UNITS // 128
DCH = 4
DCW = LOCAL // DCH
SPLIT = 96
FAR = (4, 5, 3, 6, 2, 7, 1)
I_ORDER = (0, 3, 1, 2)


def split2(v):
    hi = v.astype(bf16).astype(f32)
    return hi, v - hi


def split3(v):
    hi, rest = split2(v)
    mid, low = split2(rest)
    return hi, mid, low


def stats_rows(peak, total):
    width = peak.shape[1]
    rows = [*split3(peak), *split2(total), jnp.zeros((11, width), f32)]
    return jnp.concatenate(rows, axis=0).astype(bf16)


def read_stats(ref):
    s = ref[128:PIECE, :].astype(f32)
    return s[0:1] + s[1:2] + s[2:3], s[3:4] + s[4:5]


def wait_bytes(ref, sem):
    pltpu.make_async_copy(ref, ref, sem).wait()


def kernel(
    q_in, k_in, v_in, res_in, gain_in, wg, wu, wd, outs,
    q, k, v, res, gain, q_sem, k_sem, v_sem, res_sem, gain_sem,
    vt, sc, sbuf, xbuf, zs, zbuf, stream, ag, ginv, xn, ssb, ssc, ssr, wgu, wdv,
    gacc, gs, cbuf, ys, yb, hid, dsf, ds, dxb, zs2, dzb, fzb, fzs, fxb,
    w_sem, d_sem, ax_s, ax_r, az_s, az_r, gz_s, gz_r, gx_s, gx_r, hx_s, hx_r, hz_s, hz_r,
    sc_s, sc_r, ss_s, ss_r, c_s, c_r, y_s, y_r, hy_s, hy_r, hc_s, hc_r, dx_s, dx_r, dz_s, dz_r, fz_s, fz_r, fx_s, fx_r,
):
    kv, hd = lax.axis_index("kv"), lax.axis_index("head")
    x, z = kv // NZ, kv % NZ
    y, c = hd // 2, hd % 2

    def at_x(dx):
        return (((x + dx) % NX) * NZ + z, hd)

    def at_z(o):
        return (x * NZ + (z + o) % NZ, hd)

    def at_y(dy):
        return (kv, ((y + dy) % NY) * 2 + c)

    other = (kv, y * 2 + 1 - c)

    def remote(src, dst, send, recv, dev):
        return pltpu.make_async_remote_copy(
            src_ref=src, dst_ref=dst, send_sem=send, recv_sem=recv, device_id=dev, device_id_type=MESH
        )

    loads = [(k_in, k, k_sem), (q_in, q, q_sem), (v_in, v, v_sem), (res_in, res, res_sem), (gain_in, gain, gain_sem)]
    for src, dst, sem in loads:
        pltpu.make_async_copy(src, dst, sem).start()

    barrier = pltpu.get_barrier_semaphore()
    peers = [at_x(o) for o in range(1, NX)] + [at_z(o) for o in range(1, NZ)] + [at_y(o) for o in range(1, NY)] + [other]
    for dev in peers:
        pl.semaphore_signal(barrier, inc=1, device_id=dev, device_id_type=MESH)

    vt[HD:] = jnp.ones((16, CTX), bf16)

    def z_off(j):
        i = j % 4
        same = jnp.where(i == 0, 4, jnp.where(i == 1, 2, jnp.where(i == 2, 6, 0)))
        cross = jnp.where(i == 0, 3, jnp.where(i == 1, 5, jnp.where(i == 2, 1, 7)))
        return jnp.where((z + j // 4) % 2 == 0, same, cross)

    def z_to(j):
        return (z + z_off(j)) % NZ

    def queries_of(j):
        zt = z_to(j)
        tiles = []
        for dx in X_ORDER:
            owner = ((x + dx) % NX) * NZ + zt
            rows = q[pl.ds(pl.multiple_of(owner // 2 * 16, 16), 16), :].astype(f32)
            rows = jnp.where(zt % 2 == 0, rows[:8], rows[8:])
            tiles += [rows[:, 128 * h : 128 * h + 128] for h in range(16)]
        return jnp.concatenate(tiles, axis=0).astype(bf16)

    def scores(i, qb, top):
        rows = pl.ds(i * KC, KC)
        s = lax.dot_general(k[rows, :], qb, (((1,), (1,)), ((), ())), preferred_element_type=f32)
        sc[rows, :] = s
        m = jnp.max(s.reshape(KC // 8, 8, COLS), axis=0)
        return m if top is None else jnp.maximum(top, m)

    def add(a, b):
        return b if a is None else a + b

    def step(j, top):
        qb = queries_of((j + 1) % NZ)
        peak = jnp.max(top, axis=0, keepdims=True) * SCALE
        acc = following = None
        for i in range(CTX // KC):
            rows = pl.ds(i * KC, KC)
            p = jnp.exp2(sc[rows, :] * SCALE - peak)
            acc = add(acc, jnp.dot(vt[:, rows], p.astype(bf16), preferred_element_type=f32))
            following = scores(i, qb, following)
        stats = stats_rows(peak, acc[HD : HD + 1])
        acc = acc[:HD].astype(bf16)
        for n, dx in enumerate(X_ORDER):
            cols = slice(n * 128, n * 128 + 128)
            sbuf[dx, j, :HD, :] = acc[:, cols]
            sbuf[dx, j, HD:PIECE, :] = stats[:, cols]
        for dx in X_ORDER[:3]:
            remote(sbuf.at[dx, j], xbuf.at[dx - 1, j], ax_s, ax_r.at[dx - 1, j], at_x(dx)).start()
        return following

    def merge(refs):
        stats = [read_stats(r) for r in refs]
        peak = stats[0][0]
        for m, _ in stats[1:]:
            peak = jnp.maximum(peak, m)
        factors = [jnp.exp2(m - peak) for m, _ in stats]
        total = None
        for f, (_, t) in zip(factors, stats):
            total = add(total, f * t)
        return peak, total, factors

    def weighted(refs, weights):
        acc = None
        for r, w in zip(refs, weights):
            acc = add(acc, r[:128, :].astype(f32) * w)
        return acc

    def combine(g):
        for dx in range(1, NX):
            remote(sbuf.at[dx, g], xbuf.at[dx - 1, g], ax_s, ax_r.at[dx - 1, g], at_x(dx)).wait_recv()
        refs = [sbuf.at[0, g]] + [xbuf.at[n, g] for n in range(NX - 1)]
        peak, total, factors = merge(refs)
        zs[g, :128, :] = weighted(refs, factors).astype(bf16)
        zs[g, 128:PIECE, :] = stats_rows(peak, total)
        off = z_off(g)

        @pl.when(off != 0)
        def _():
            remote(zs.at[g], zbuf.at[off - 1], az_s, az_r.at[off - 1], at_z(off)).start()

    for src, dst, sem in loads[:2]:
        pltpu.make_async_copy(src, dst, sem).wait()
    first = queries_of(0)
    top = None
    for i in range(CTX // KC):
        top = scores(i, first, top)
    for src, dst, sem in loads[2:]:
        pltpu.make_async_copy(src, dst, sem).wait()
    for j in range(FCH):
        cols = pl.ds(j * 128, 128)
        pltpu.make_async_copy(wg.at[:, cols], wgu.at[j, :, pl.ds(0, 128)], w_sem).start()
        pltpu.make_async_copy(wu.at[:, cols], wgu.at[j, :, pl.ds(128, 128)], w_sem).start()
    for j in range(DCH):
        pltpu.make_async_copy(wd.at[:, pl.ds(j * DCW, DCW)], wdv.at[j], d_sem).start()

    vt[:HD] = v[...].astype(f32).T.astype(bf16)

    pl.semaphore_wait(barrier, len(peers))

    def gather_z(o):
        return remote(part(kv), part(kv), gz_s, gz_r.at[o - 1], at_z(o))

    def part(src):
        return ag.at[src, pl.ds(0, SPLIT)]

    def rest(src):
        return ag.at[src, pl.ds(SPLIT, 128 - SPLIT)]

    def rest_x(src, dx):
        return remote(rest(src), rest(src), hx_s, hx_r.at[dx - 1], at_x(dx))

    def rest_z(src):
        for o in FAR:
            remote(rest(src), rest(src), hz_s, hz_r.at[o - 1], at_z(o)).start()

    def pass_rest(p):
        @pl.when(z % 2 == p)
        def _():
            rest_z(kv)
            for dx in (1, 3, 2):
                src = ((x + NX - dx) % NX) * NZ + z
                rest_x(src, dx).wait_recv()
                rest_z(src)

    def finish_merge(p):
        @pl.when(z % 2 == p)
        def _():
            for o in range(1, NZ):
                remote(zs.at[0], zbuf.at[o - 1], az_s, az_r.at[o - 1], at_z(o)).wait_recv()
            refs = [zs.at[4 * p + 3]] + [zbuf.at[n] for n in range(NZ - 1)]
            _, total, factors = merge(refs)
            inv = 1.0 / total
            att = weighted(refs, [f * inv for f in factors]).T
            att = jnp.concatenate([att[8 * h : 8 * h + 8, :] for h in range(16)], axis=1).astype(bf16)
            outs[0] = att
            st = res[...].astype(f32) + att.astype(f32)
            stream[...] = st
            t = st * gain[...]
            rows = jnp.concatenate([t[:, 128 * h : 128 * h + 128] for h in range(16)], axis=0)
            ag[kv] = rows.astype(bf16)
            for o in FAR:
                gather_z(o).start()
            for dx in (2, 1, 3):
                rest_x(kv, dx).start()

    def attend(j, top):
        top = step(j, top)

        @pl.when(j >= 3)
        def _():
            combine(j - 3)

        return top

    lax.fori_loop(0, NZ, attend, top)

    def gather_x(src, dx, recv):
        return remote(part(src), part(src), gx_s, recv, at_x(dx))

    def source(p, i):
        o = 2 * i + (z + p) % 2
        return o, (z + NZ - o) % NZ

    def spread(p, i):
        o, zo = source(p, i)
        src = x * NZ + zo

        @pl.when(o != 0)
        def _():
            remote(part(src), part(src), gz_s, gz_r.at[o - 1], at_z(o)).wait_recv()

        for dx in (2, 1, 3):
            gather_x(src, dx, gx_r.at[dx - 1, o]).start()

    def gathered(p):
        for i in I_ORDER:
            o, zo = source(p, i)
            for dx in range(1, NX):
                gather_x(((x + NX - dx) % NX) * NZ + zo, dx, gx_r.at[dx - 1, o]).wait_recv()

            @pl.when(o != 0)
            def _():
                wait_bytes(ag.at[pl.ds(0, NX), pl.ds(SPLIT, 128 - SPLIT)], hz_r.at[o - 1])

    def row_squares(rows):
        st = rows * ginv[...]
        return jnp.sum((st * st).reshape(16, OWN, 128), axis=0)

    def rebuild(p):
        def pair(i, _):
            first = (i // 2) * NZ + 4 * (i % 2) + p
            a = ag[first].astype(f32)
            b = ag[first + 2].astype(f32)
            rows = pl.ds(pl.multiple_of(i * 16, 16), 16)
            for h in range(16):
                tile = jnp.concatenate([a[8 * h : 8 * h + 8], b[8 * h : 8 * h + 8]], axis=0)
                xn[p, rows, 128 * h : 128 * h + 128] = tile.astype(bf16)
            ssb[p, rows, :] = jnp.concatenate([row_squares(a), row_squares(b)], axis=0)
            return 0

        lax.fori_loop(0, 8, pair, 0)

    mine = pl.ds(pl.multiple_of(c * 64, 64), 64)
    theirs = pl.ds(pl.multiple_of((1 - c) * 64, 64), 64)

    def rows_at(yy, cc):
        return pl.ds(pl.multiple_of((cc * NY + yy) * 16, 16), 16)

    own16 = rows_at(y, c)

    def square_core(p):
        return remote(ssb.at[p, theirs], ssc.at[p], sc_s, sc_r.at[p], other)

    def square_y(p, dy):
        src = ssb.at[p, rows_at((y + dy) % NY, c)]
        return remote(src, ssr.at[p, dy - 1], ss_s, ss_r.at[p, dy - 1], at_y(dy))

    def core_copy(p, j):
        return remote(gs.at[p, j], cbuf.at[p, j], c_s, c_r.at[p, j], other)

    def project(p):
        square_core(p).start()

        def chunk(j, _):
            gacc[p, j] = jnp.dot(xn[p], wgu[j], preferred_element_type=f32)
            gs[p, j] = gacc[p, j, theirs, :].astype(bf16)
            core_copy(p, j).start()
            return 0

        lax.fori_loop(0, FCH, chunk, 0)

    def sum_cores(p):
        square_core(p).wait_recv()
        ssb[p, mine, :] = ssb[p, mine, :] + ssc[p]
        for dy in (2, 1, 3):
            square_y(p, dy).start()

        def chunk(j, _):
            core_copy(p, j).wait_recv()
            s = gacc[p, j, mine, :] + cbuf[p, j].astype(f32)
            gacc[p, j, mine, :] = s
            ys[p, j] = s.astype(bf16).reshape(NY, 16, 256)
            for dy in (2, 1, 3):
                to = (y + dy) % NY
                remote(ys.at[p, j, to], yb.at[p, dy - 1, j], y_s, y_r.at[p, dy - 1], at_y(dy)).start()
            return 0

        lax.fori_loop(0, FCH, chunk, 0)

    def hid_rows(p, yy):
        return hid.at[p, rows_at(yy, c)]

    def hid_y(p, yy, dy):
        return remote(hid_rows(p, yy), hid_rows(p, yy), hy_s, hy_r.at[p, dy - 1], at_y(dy))

    def hid_core(p, yy):
        return remote(hid_rows(p, yy), hid_rows(p, yy), hc_s, hc_r.at[p], other)

    def activate(p):
        for dy in range(1, NY):
            square_y(p, dy).wait_recv()
        squares = ssb[p, own16, :]
        for n in range(NY - 1):
            squares = squares + ssr[p, n]
        scale = lax.rsqrt(jnp.sum(squares, axis=1, keepdims=True) / D + EPSILON)
        for dy in range(1, NY):
            wait_bytes(yb.at[p, dy - 1], y_r.at[p, dy - 1])
        for j in range(FCH):
            s = gacc[p, j, own16, :]
            for n in range(NY - 1):
                s = s + yb[p, n, j].astype(f32)
            gate = s[:, :128] * scale
            up = s[:, 128:] * scale
            hid[p, own16, 128 * j : 128 * j + 128] = (gate / (1.0 + jnp.exp(-gate)) * up).astype(bf16)
        for dy in (2, 1, 3):
            hid_y(p, y, dy).start()
        hid_core(p, y).start()

    def hid_forward(p):
        for dy in (1, 3, 2):
            yy = (y + NY - dy) % NY
            hid_y(p, yy, dy).wait_recv()
            hid_core(p, yy).start()

    def down_x(p, j, dx):
        src = ds.at[p, j, (x + dx) % NX]
        return remote(src, dxb.at[p, dx - 1, j], dx_s, dx_r.at[p, dx - 1, j], at_x(dx))

    def down(p):
        wait_bytes(hid.at[p, theirs], hc_r.at[p])

        def chunk(j):
            acc = jnp.dot(hid[p], wdv[j], preferred_element_type=f32)
            for h in range(DCW // 128):
                dsf[:, h] = acc[:, 128 * h : 128 * h + 128].reshape(NKV // 2, OWN, 128)
            ds[p, j] = dsf[...].reshape(NX, 128, 128).astype(bf16)

        chunk(0)
        for n in range(4):
            off, i = owner_of(p, n)

            @pl.when(off != 0)
            def _():
                src = ds.at[p, 0, :, pl.ds(pl.multiple_of(32 * i, 32), 32)]
                remote(src, fzb.at[off - 1], fz_s, fz_r.at[off - 1], at_z(off)).start()

        def later(j, _):
            chunk(j)
            for dx in (2, 1, 3):
                down_x(p, j, dx).start()
            return 0

        lax.fori_loop(1, DCH, later, 0)

    def owner_of(p, n):
        off = z_off(4 * p + n)
        return off, ((z + off) % NZ) // 2

    def sum_z(p):
        @pl.when(z % 2 == p)
        def _():
            for o in range(1, NZ):
                remote(fzb.at[o - 1], fzb.at[o - 1], fz_s, fz_r.at[o - 1], at_z(o)).wait_recv()
            s = ds[p, 0, :, pl.ds(pl.multiple_of(z // 2 * 32, 32), 32), :].astype(f32)
            for n in range(NZ - 1):
                s = s + fzb[n].astype(f32)
            fzs[...] = s.astype(bf16)
            for dx in (2, 1, 3):
                last_x(dx).start()

    def last_x(dx):
        return remote(fzs.at[(x + dx) % NX], fxb.at[dx - 1], fx_s, fx_r.at[dx - 1], at_x(dx))

    def sum_x(p):
        def chunk(j, _):
            for dx in range(1, NX):
                down_x(p, j, dx).wait_recv()
            s = ds[p, j, x].astype(f32)
            for n in range(NX - 1):
                s = s + dxb[p, n, j].astype(f32)
            zs2[p, j] = s.astype(bf16).reshape(4, 32, 128)
            for n in range(4):
                off, i = owner_of(p, n)

                @pl.when(off != 0)
                def _():
                    remote(
                        zs2.at[p, j, i], dzb.at[off - 1, j - 1], dz_s, dz_r.at[off - 1], at_z(off)
                    ).start()

            return 0

        lax.fori_loop(1, DCH, chunk, 0)

    def finish(p):
        @pl.when(z % 2 == p)
        def _():
            for dx in range(1, NX):
                last_x(dx).wait_recv()
            for o in range(1, NZ):
                wait_bytes(dzb.at[o - 1], dz_r.at[o - 1])
            for j in range(DCH):
                if j == 0:
                    s = fzs[x].astype(f32)
                    for n in range(NX - 1):
                        s = s + fxb[n].astype(f32)
                else:
                    s = zs2[p, j, z // 2].astype(f32)
                    for n in range(NZ - 1):
                        s = s + dzb[n, j - 1].astype(f32)
                s = jnp.concatenate([s[8 * h : 8 * h + 8] for h in range(DCW // 128)], axis=1)
                cols = slice(j * DCW, j * DCW + DCW)
                outs[1, :, cols] = (stream[:, cols] + s).astype(bf16)

    finish_merge(0)
    combine(5)
    combine(6)
    combine(7)
    finish_merge(1)
    for i in I_ORDER:
        spread(0, i)
    pass_rest(0)
    pass_rest(1)
    inverse = jnp.broadcast_to(1.0 / gain[...], (OWN, LOCAL))
    ginv[...] = jnp.concatenate([inverse[:, 128 * h : 128 * h + 128] for h in range(16)], axis=0)
    for i in I_ORDER:
        spread(1, i)
    gathered(0)
    rebuild(0)
    wait_bytes(wgu, w_sem)
    project(0)
    sum_cores(0)
    gathered(1)
    rebuild(1)
    project(1)
    activate(0)
    sum_cores(1)
    hid_forward(0)
    wait_bytes(wdv, d_sem)
    activate(1)
    down(0)
    hid_forward(1)
    down(1)
    sum_z(0)
    sum_x(0)
    sum_x(1)
    sum_z(1)
    finish(0)
    finish(1)

    wait_bytes(sbuf.at[pl.ds(1, 3)], ax_s)
    wait_bytes(zs.at[pl.ds(0, 7)], az_s)
    wait_bytes(ag.at[pl.ds(0, 7), pl.ds(0, SPLIT)], gz_s)
    wait_bytes(ag.at[pl.ds(0, 24), pl.ds(0, SPLIT)], gx_s)
    wait_bytes(ag.at[pl.ds(0, 3), pl.ds(SPLIT, 128 - SPLIT)], hx_s)
    wait_bytes(ag.at[pl.ds(0, 28), pl.ds(SPLIT, 128 - SPLIT)], hz_s)
    wait_bytes(ssc, sc_s)
    wait_bytes(ssr, ss_s)
    wait_bytes(gs, c_s)
    wait_bytes(yb, y_s)
    wait_bytes(hid.at[0, pl.ds(0, 96)], hy_s)
    wait_bytes(hid.at[0], hc_s)
    wait_bytes(dxb.at[:, :, pl.ds(1, DCH - 1)], dx_s)
    wait_bytes(fzb, fz_s)
    wait_bytes(fxb, fx_s)
    wait_bytes(dzb, dz_s)


def body(queries, cache_keys, cache_values, residual, norm_gain, w_gate, w_up, w_down):
    vmem = pl.BlockSpec(memory_space=pltpu.VMEM)
    hbm = pl.BlockSpec(memory_space=pl.ANY)
    dma = pltpu.SemaphoreType.DMA
    shape = pltpu.VMEM((2, OWN, LOCAL), bf16)
    scratch = [
        pltpu.VMEM((256, LOCAL), bf16),
        pltpu.VMEM((CTX, HD), bf16),
        pltpu.VMEM((CTX, HD), bf16),
        pltpu.VMEM((OWN, LOCAL), bf16),
        pltpu.VMEM((1, LOCAL), f32),
        dma, dma, dma, dma, dma,
        pltpu.VMEM((HD + 16, CTX), bf16),
        pltpu.VMEM((CTX, COLS), f32),
        pltpu.VMEM((NX, NZ, PIECE, 128), bf16),
        pltpu.VMEM((NX - 1, NZ, PIECE, 128), bf16),
        pltpu.VMEM((NZ, PIECE, 128), bf16),
        pltpu.VMEM((NZ - 1, PIECE, 128), bf16),
        pltpu.VMEM((OWN, LOCAL), f32),
        pltpu.VMEM((NKV, 128, 128), bf16),
        pltpu.VMEM((128, 128), f32),
        pltpu.VMEM((2, 128, LOCAL), bf16),
        pltpu.VMEM((2, 128, 128), f32),
        pltpu.VMEM((2, 64, 128), f32),
        pltpu.VMEM((2, NY - 1, 16, 128), f32),
        pltpu.VMEM((FCH, LOCAL, 256), bf16),
        pltpu.VMEM((DCH, UNITS, DCW), bf16),
        pltpu.VMEM((2, FCH, 128, 256), f32),
        pltpu.VMEM((2, FCH, 64, 256), bf16),
        pltpu.VMEM((2, FCH, 64, 256), bf16),
        pltpu.VMEM((2, FCH, NY, 16, 256), bf16),
        pltpu.VMEM((2, NY - 1, FCH, 16, 256), bf16),
        pltpu.VMEM((2, 128, UNITS), bf16),
        pltpu.VMEM((NKV // 2, DCW // 128, OWN, 128), f32),
        pltpu.VMEM((2, DCH, NX, 128, 128), bf16),
        pltpu.VMEM((2, NX - 1, DCH, 128, 128), bf16),
        pltpu.VMEM((2, DCH, 4, 32, 128), bf16),
        pltpu.VMEM((NZ - 1, DCH - 1, 32, 128), bf16),
        pltpu.VMEM((NZ - 1, NX, 32, 128), bf16),
        pltpu.VMEM((NX, 32, 128), bf16),
        pltpu.VMEM((NX - 1, 32, 128), bf16),
        dma, dma,
        dma, dma((NX - 1, NZ)),
        dma, dma((NZ - 1,)),
        dma, dma((NZ - 1,)),
        dma, dma((NX - 1, NZ)),
        dma, dma((NX - 1,)),
        dma, dma((NZ - 1,)),
        dma, dma((2,)),
        dma, dma((2, NY - 1)),
        dma, dma((2, FCH)),
        dma, dma((2, NY - 1)),
        dma, dma((2, NY - 1)),
        dma, dma((2,)),
        dma, dma((2, NX - 1, DCH)),
        dma, dma((NZ - 1,)),
        dma, dma((NZ - 1,)),
        dma, dma((NX - 1,)),
    ]
    outs = pl.pallas_call(
        kernel,
        out_shape=shape,
        in_specs=[hbm] * 8,
        out_specs=vmem,
        scratch_shapes=scratch,
        name="layer",
        compiler_params=pltpu.CompilerParams(
            collective_id=0, has_side_effects=True, vmem_limit_bytes=56 * 2**20
        ),
    )(
        queries, cache_keys, cache_values, residual, norm_gain.reshape(1, LOCAL), w_gate, w_up, w_down
    )
    return outs[0], outs[1]


def solution(mesh):
    in_specs = (
        P(None, "head"),
        P("kv", "head"),
        P("kv", "head"),
        P("kv", "head"),
        P("head"),
        P("head", "kv"),
        P("head", "kv"),
        P("kv", "head"),
    )
    out_specs = (P("kv", "head"), P("kv", "head"))
    return jax.shard_map(body, mesh=mesh, in_specs=in_specs, out_specs=out_specs, check_vma=False)
```
